512 devices in a mesh: section: 32 (over y, z_lo, core), seq: 16 (over x, z_hi).
Axes of the slice: x: 4, y: 8, z: 8 (z_hi: 4, z_lo: 2; z = z_hi * 2 + z_lo), core: 2. Of those that a mesh axis runs over, the one named last changes fastest.
Arguments:
- latents: bfloat16 [32, 512, 3072], P('section', None, 'seq'), may hold values from -400 to 400
- patch_order: int32 [8], replicated, may hold values from 0 to 7, each once
- timestep: int32 [1], replicated, may hold values from 0 to 63
- mod_table: float32 [64, 32, 3, 3072], P(None, 'section', None, 'seq'), may hold values from -4 to 4
- w_qkv: bfloat16 [32, 3072, 3, 2048], P('section', None, None, 'seq'), may hold values from -0.36084392 to 0.36084392
- w_out: bfloat16 [32, 2048, 3072], P('section', None, 'seq'), may hold values from -0.125 to 0.125
- kv_cache: bfloat16 [32, 2, 512, 2048], P('section', None, None, 'seq'), may hold values from -9 to 9
Outputs:
- block_out: bfloat16 [32, 512, 3072], P('section', None, 'seq')
- cache_out: bfloat16 [32, 2, 512, 2048], P('section', None, None, 'seq')
The draws below stay inside these ranges and needn't reach their ends.
Inputs may be any that keep to these rules, and one draw needn't show every extreme that they name: `patch_order`: each of the 8 patches once.
All inputs are finite; a program needn't handle non-finite values.
Results may differ from the reference program's by a relative error of at most 0.015.
Values may be sent and summed in bfloat16 or wider, within the bound.
No kernel may reach another device: no remote copies, remote signals or barrier semaphores. Data moves between devices by JAX's collectives and lax.ppermute only.
A program may use at most 64 MiB of HBM per device.

```python
import jax
import jax.numpy as jnp
from jax import lax

D = 3072
HEAD_DIM = 128
HEADS = 16
PATCHES = 8
PATCH_ROWS = 64
NT = 64
CHAIN = 4
SECTIONS = 32
ATT = 2048
LEN = 512


def draw_latents(key, part):
    key = jax.random.fold_in(key, 11)
    subkeys = jax.random.split(key, 1)
    col_ramp = jnp.exp(jnp.log(3.0) * jnp.arange(D, dtype=jnp.float32) / D)
    standard = jnp.clip(jax.random.normal(subkeys[0], (SECTIONS, LEN, D), jnp.float32), -4.0, 4.0)
    drawn = standard * col_ramp
    return drawn.astype(jnp.bfloat16)


def draw_w_qkv(key, part):
    key = jax.random.fold_in(key, 23)
    subkeys = jax.random.split(key, 1)
    spread = D ** (-0.5)
    standard = jnp.clip(jax.random.normal(subkeys[0], (SECTIONS, D, 3, ATT), jnp.float32), -4.0, 4.0) * spread
    factor = jnp.array([1.4, 1.4, 1.0], jnp.float32)[None, None, :, None]
    weights = standard * factor
    return weights.astype(jnp.bfloat16)


def steps_of(own_key, dims, shards, least, high):
    def one(position, blocks):
        draws = jax.random.uniform(jax.random.fold_in(jax.random.fold_in(own_key, 6), position), (blocks,), jnp.float32, least / len(shards), high / len(shards))
        return jnp.repeat(jnp.exp(draws), dims[position] // blocks).reshape((-1,) + (1,) * (len(dims) - position - 1))

    factor_of = one(*shards[0])
    for cut in shards[1:]:
        factor_of = factor_of * one(*cut)
    return factor_of


def gaussian(key, extent, width, limit, cuts=(), held_as=jnp.bfloat16):
    entries = width * jax.random.normal(key, extent, jnp.float32)
    if cuts:
        entries = entries * steps_of(key, extent, cuts, -0.22, 0.18)
    return jnp.clip(entries, -limit, limit).astype(held_as)


def setup_inputs(seed: int = 0) -> dict:
    arg_keys = jax.random.split(jax.random.key(seed), 8)
    return {
        "latents": draw_latents(jax.random.fold_in(arg_keys[7], 71), 0),
        "patch_order": jax.random.permutation(arg_keys[1], PATCHES).astype(jnp.int32),
        "timestep": jax.random.randint(arg_keys[2], (1,), 0, NT).astype(jnp.int32),
        "mod_table": gaussian(arg_keys[3], (NT, SECTIONS, 3, D), 0.7, 4.0, ((1, 32), (3, 16)), jnp.float32),
        "w_qkv": draw_w_qkv(jax.random.fold_in(arg_keys[7], 71), 0),
        "w_out": gaussian(arg_keys[5], (SECTIONS, ATT, D), ATT ** -0.5, 0.125, ((0, 32), (2, 16))),
        "kv_cache": gaussian(arg_keys[6], (SECTIONS, 2, LEN, ATT), 1.5, 9.0, ((0, 32), (3, 16))),
    }


EPSILON = 1e-06

def section_block(stream, kv_start, w_block, w_proj, mod_block, patch_order):
    w_flat = w_block.reshape(D, 3 * ATT)

    def one_patch(running, patch_id):
        kv_store, out_rows = running
        row_start = (patch_id * PATCH_ROWS).astype(jnp.int32)
        anchor = jnp.zeros((), jnp.int32)
        rows_f = lax.dynamic_slice_in_dim(stream, row_start, PATCH_ROWS, 0).astype(jnp.float32)
        row_mean = lax.optimization_barrier(jnp.sum(rows_f, axis=1, keepdims=True)) / D
        row_var = lax.optimization_barrier(jnp.sum(rows_f * rows_f, axis=1, keepdims=True)) / D - row_mean * row_mean
        normed = ((rows_f - row_mean) * lax.rsqrt(row_var + EPSILON) * (1.0 + mod_block[1]) + mod_block[0]).astype(jnp.bfloat16)
        triple = jnp.dot(normed, w_flat, preferred_element_type=jnp.float32).astype(jnp.bfloat16)
        triple = triple.reshape(PATCH_ROWS, 3, ATT)
        fresh_kv = jnp.stack([triple[:, 1], triple[:, 2]])
        kv_store = lax.dynamic_update_slice(kv_store, fresh_kv, (anchor, row_start, anchor))
        queries = triple[:, 0].reshape(PATCH_ROWS, HEADS, HEAD_DIM).astype(jnp.float32)
        cached_keys = kv_store[0].reshape(LEN, HEADS, HEAD_DIM).astype(jnp.float32)
        values = kv_store[1].reshape(LEN, HEADS, HEAD_DIM).astype(jnp.float32)
        scores = jnp.einsum('rhd,lhd->hrl', queries, cached_keys) * HEAD_DIM ** (-0.5)
        row_top = lax.optimization_barrier(jnp.max(scores, axis=2, keepdims=True))
        exp_terms = jnp.exp(scores - row_top)
        weights_bf = (exp_terms / lax.optimization_barrier(jnp.sum(exp_terms, axis=2, keepdims=True))).astype(jnp.bfloat16)
        mixed = jnp.einsum('hrl,lhd->rhd', weights_bf.astype(jnp.float32), values)
        mixed = mixed.astype(jnp.bfloat16).reshape(PATCH_ROWS, ATT)
        projection = jnp.dot(mixed, w_proj, preferred_element_type=jnp.float32)
        result = (rows_f + mod_block[2] * projection).astype(jnp.bfloat16)
        out_rows = lax.dynamic_update_slice(out_rows, result, (row_start, anchor))
        return ((kv_store, out_rows), None)
    (kv_store, out_rows), _ = lax.scan(one_patch, (kv_start, jnp.zeros_like(stream)), patch_order)
    return (out_rows, kv_store)

def reference(latents, patch_order, timestep, mod_table, w_qkv, w_out, kv_cache):
    mod_rows = mod_table[timestep[0]]
    block_ids = jnp.arange(SECTIONS, dtype=jnp.int32)

    def one_section(stream, inputs):
        mod_block, w_block, w_proj, kv_start, stale, block_id = inputs
        source = jnp.where(block_id % CHAIN == 0, stale, stream)
        out_rows, kv_store = section_block(source, kv_start, w_block, w_proj, mod_block, patch_order)
        return (out_rows, (out_rows, kv_store))
    _, (section_outs, caches) = lax.scan(one_section, latents[0], (mod_rows, w_qkv, w_out, kv_cache, latents, block_ids))
    return (section_outs, caches)
```

```python
import functools

import jax
import jax.numpy as jnp
from jax import lax
from jax.experimental import pallas as pl
from jax.experimental.pallas import tpu as pltpu
from jax.sharding import PartitionSpec as P

HEAD_DIM = 128
PATCHES = 8
CHAIN = 4
EPSILON = 1e-06
ROWS = 64
GROUP = PATCHES // 2
HALF = GROUP * ROWS
LANES = 128
REST = 64
SHARD = LANES + REST
PACK = HALF + HALF // 2
MODS = 16
F32 = jnp.float32
BF16 = jnp.bfloat16
VMEM = pl.BlockSpec(memory_space=pltpu.VMEM)
SMEM = pl.BlockSpec(memory_space=pltpu.SMEM)
ANY = pl.BlockSpec(memory_space=pl.ANY)


def params():
    return pltpu.CompilerParams(vmem_limit_bytes=20 * 1024 * 1024)


def low_lanes(rows):
    return lax.broadcasted_iota(jnp.int32, (rows, LANES), 1) < REST


def patch_at(order_ref, j):
    return pl.ds(pl.multiple_of(order_ref[j] * ROWS, ROWS), ROWS)


def pack_kernel(order_ref, lat_ref, mod_ref, own_ref, send_ref, rows_ref):
    rows_ref[:, :SHARD] = lat_ref[...].astype(F32).T
    low = low_lanes(ROWS)
    for group, out in ((0, own_ref), (1, send_ref)):
        rest = []
        for j in range(GROUP):
            at = patch_at(order_ref, group * GROUP + j)
            out[j * ROWS : (j + 1) * ROWS, :] = rows_ref[at, :LANES].astype(BF16)
            rest.append(rows_ref[at, LANES:])
        for j in range(2):
            both = jnp.where(low, rest[j], pltpu.roll(rest[j + 2], REST, 1))
            out[HALF + j * ROWS : HALF + (j + 1) * ROWS, :] = both.astype(BF16)
    mod = mod_ref[...]
    kinds = (1.0 + mod[1:2], mod[0:1], mod[2:3])
    lines = []
    for kind in kinds:
        first = kind[:, :LANES]
        last = jnp.concatenate([kind[:, LANES:], kind[:, LANES:]], axis=1)
        for value in (first, last):
            high = value.astype(BF16).astype(F32)
            lines += [high, value - high]
    lines.append(jnp.zeros((MODS - len(lines), LANES), F32))
    send_ref[PACK:, :] = jnp.concatenate(lines, axis=0).astype(BF16)


def spread_kernel(copies, x_ref, mods_ref, out_ref):
    for s in range(copies):
        out_ref[s, :PACK, :] = x_ref[...]
        out_ref[s, PACK:, :] = mods_ref[...]


def project_kernel(sources, flag_ref, x_ref, own_ref, peer_ref, q_ref, kv_ref, wm_ref, wr_ref, nm_ref, nr_ref, sems):
    def copies(w_ref):
        found = []
        for t in range(3):
            lanes = pl.ds(t * HEAD_DIM, HEAD_DIM)
            found.append(pltpu.make_async_copy(w_ref.at[t, :, :LANES, :], wm_ref.at[:, :, lanes], sems.at[2 * t]))
            found.append(pltpu.make_async_copy(w_ref.at[t, :, LANES:, :], wr_ref.at[:, :, lanes], sems.at[2 * t + 1]))
        return found

    @pl.when(flag_ref[0] == 1)
    def _():
        for copy in copies(own_ref):
            copy.start()

    @pl.when(flag_ref[0] == 0)
    def _():
        for copy in copies(peer_ref):
            copy.start()

    width = sources * SHARD
    low = low_lanes(ROWS)

    def line(s, k):
        at = PACK + 2 * k
        pair = x_ref[s, PACK:, :].astype(F32)
        return pair[2 * k : 2 * k + 1] + pair[2 * k + 1 : 2 * k + 2]

    scale_first = [line(s, 0) for s in range(sources)]
    shift_first = [line(s, 2) for s in range(sources)]
    scale_last = [jnp.where(low[:1], line(2 * p, 1), line(2 * p + 1, 1)) for p in range(sources // 2)]
    shift_last = [jnp.where(low[:1], line(2 * p, 3), line(2 * p + 1, 3)) for p in range(sources // 2)]
    for j in range(GROUP):
        mine = pl.ds(j * ROWS, ROWS)
        rest = pl.ds(HALF + (j % 2) * ROWS, ROWS)
        total = jnp.zeros((ROWS, LANES), F32)
        square = jnp.zeros((ROWS, LANES), F32)
        total_rest = jnp.zeros((ROWS, LANES), F32)
        square_rest = jnp.zeros((ROWS, LANES), F32)
        for s in range(sources):
            x = x_ref[s, mine, :].astype(F32)
            total = total + x
            square = square + x * x
            x = x_ref[s, rest, :].astype(F32)
            total_rest = total_rest + x
            square_rest = square_rest + x * x
        in_half = low if j < 2 else jnp.logical_not(low)
        total = total + jnp.where(in_half, total_rest, 0.0)
        square = square + jnp.where(in_half, square_rest, 0.0)
        mean = jnp.sum(total, axis=1, keepdims=True) / width
        var = jnp.sum(square, axis=1, keepdims=True) / width - mean * mean
        rstd = lax.rsqrt(var + EPSILON)
        for s in range(sources):
            x = x_ref[s, mine, :].astype(F32)
            normed = (x - mean) * rstd * scale_first[s] + shift_first[s]
            nm_ref[mine, s * LANES : (s + 1) * LANES] = normed.astype(BF16)
        for p in range(sources // 2):
            even = x_ref[2 * p, rest, :].astype(F32)
            odd = x_ref[2 * p + 1, rest, :].astype(F32)
            if j < 2:
                x = jnp.where(low, even, pltpu.roll(odd, REST, 1))
            else:
                x = jnp.where(low, pltpu.roll(even, REST, 1), odd)
            normed = (x - mean) * rstd * scale_last[p] + shift_last[p]
            nr_ref[mine, p * LANES : (p + 1) * LANES] = normed.astype(BF16)

    for copy in copies(own_ref):
        copy.wait()
    w_first = wm_ref[...].reshape(sources * LANES, 3 * HEAD_DIM)
    w_last = wr_ref[...].reshape(sources * REST, 3 * HEAD_DIM)
    qkv = jnp.dot(nm_ref[...], w_first, preferred_element_type=F32)
    qkv = qkv + jnp.dot(nr_ref[...], w_last, preferred_element_type=F32)
    qkv = qkv.astype(BF16)
    q_ref[...] = qkv[:, :HEAD_DIM]
    kv_ref[0] = qkv[:, HEAD_DIM : 2 * HEAD_DIM]
    kv_ref[1] = qkv[:, 2 * HEAD_DIM :]


def attend_kernel(copies, flag_ref, order_ref, q_ref, kv_ref, other_ref, own_ref, peer_ref, out_ref):
    mine = flag_ref[0] == 1
    core = flag_ref[1]

    def stale(part, j):
        at = patch_at(order_ref, j)
        return jnp.where(mine, own_ref[part, at, :], peer_ref[part, at, :])

    old, other = [], []
    for part in range(2):
        old.append([stale(part, core * GROUP + j) for j in range(GROUP)])
        kept = jnp.concatenate([stale(part, (1 - core) * GROUP + j) for j in range(GROUP)], axis=0)
        other.append(jnp.where(core == 1, other_ref[part], kept))
    for j in range(GROUP):
        at = slice(j * ROWS, (j + 1) * ROWS)
        keys, values = (
            jnp.concatenate([kv_ref[part, : (j + 1) * ROWS, :]] + old[part][j + 1 :] + [other[part]], axis=0)
            for part in range(2)
        )
        scores = lax.dot_general(q_ref[at, :], keys, (((1,), (1,)), ((), ())), preferred_element_type=F32)
        scores = scores * HEAD_DIM ** (-0.5)
        terms = jnp.exp(scores - jnp.max(scores, axis=1, keepdims=True))
        weights = (terms / jnp.sum(terms, axis=1, keepdims=True)).astype(BF16)
        mixed = jnp.dot(weights, values, preferred_element_type=F32).astype(BF16)
        for s in range(copies):
            out_ref[s, at, :] = mixed


def update_kernel(heads, last, flag_ref, mixed_ref, own_ref, peer_ref, x_ref, mods_ref, *refs):
    if last:
        next_ref, (new_ref, w_ref, held_ref, sem) = None, refs
    else:
        next_ref, new_ref, spread_ref, w_ref, held_ref, sem = refs

    @pl.when(flag_ref[0] == 1)
    def _():
        pltpu.make_async_copy(own_ref, w_ref, sem).start()

    @pl.when(flag_ref[0] == 0)
    def _():
        pltpu.make_async_copy(peer_ref, w_ref, sem).start()

    mixed = jnp.concatenate([mixed_ref[h] for h in range(heads)], axis=1)
    pltpu.make_async_copy(own_ref, w_ref, sem).wait()
    held_ref[:, :SHARD] = lax.dot_general(mixed, w_ref[...], (((1,), (1,)), ((), ())), preferred_element_type=F32)
    mods = mods_ref[...].astype(F32)
    gate_first = mods[8:9] + mods[9:10]
    gate_last = mods[10:11] + mods[11:12]
    first = x_ref[:HALF, :].astype(F32) + gate_first * held_ref[:, :LANES]
    rest = jnp.where(
        low_lanes(HALF // 2), held_ref[: HALF // 2, LANES:], pltpu.roll(held_ref[HALF // 2 :, LANES:], REST, 1)
    )
    rest = x_ref[HALF:, :].astype(F32) + gate_last * rest
    first, rest = first.astype(BF16), rest.astype(BF16)
    new_ref[:HALF, :] = first
    new_ref[HALF:, :] = rest
    if not last:
        for s in range(heads):
            spread_ref[s, :HALF, :] = first
            spread_ref[s, HALF:PACK, :] = rest
            spread_ref[s, PACK:, :] = next_ref[...]


def finish_kernel(flag_ref, order_ref, mine_ref, other_ref, kv_ref, kv_other_ref, out_ref, cache_ref, rows_ref):
    core = flag_ref[0]
    for whose, (x_ref, new_ref) in enumerate(((mine_ref, kv_ref), (other_ref, kv_other_ref))):
        group = core if whose == 0 else 1 - core
        for j in range(GROUP):
            at = patch_at(order_ref, group * GROUP + j)
            here = slice(j * ROWS, (j + 1) * ROWS)
            rest = x_ref[HALF + (j % 2) * ROWS : HALF + (j % 2 + 1) * ROWS, :].astype(F32)
            rows_ref[at, :LANES] = x_ref[here, :].astype(F32)
            rows_ref[at, LANES:] = rest if j < 2 else pltpu.roll(rest, REST, 1)
            for part in range(2):
                cache_ref[part, at, :] = new_ref[part, here, :]
    out_ref[...] = rows_ref[...].T[:SHARD, :].astype(BF16)


def body(latents, patch_order, timestep, mod_table, w_qkv, w_out, kv_cache):
    sections, seq = lax.axis_size("section"), lax.axis_size("seq")
    section = lax.axis_index("section")
    core = (section % 2).astype(jnp.int32)
    second = (section // 2) % 2
    swap_pairs = [(i, i ^ 1) for i in range(sections)]
    hop_pairs = [(i, i + 2) for i in range(sections) if i % CHAIN < 2]

    def swap(value):
        return lax.ppermute(value, "section", swap_pairs)

    def everyone(spread):
        return lax.all_to_all(spread, "seq", 0, 0)

    def shaped(*shape, dtype=BF16):
        return jax.ShapeDtypeStruct(shape, dtype)

    w_own = jnp.transpose(w_qkv[0], (1, 0, 2))
    o_own = jnp.transpose(w_out[0], (1, 0))
    cache_own = kv_cache[0]
    mod_now = lax.dynamic_index_in_dim(mod_table, timestep[0], 0, keepdims=False)[0]
    width = w_own.shape[1]

    own, send = pl.pallas_call(
        pack_kernel,
        out_shape=(shaped(PACK, LANES), shaped(PACK + MODS, LANES)),
        in_specs=[SMEM, VMEM, VMEM],
        out_specs=(VMEM, VMEM),
        scratch_shapes=[pltpu.VMEM((PATCHES * ROWS, 2 * LANES), F32)],
        compiler_params=params(),
        name="pack",
    )(patch_order, jnp.transpose(latents[0], (1, 0)), mod_now)
    got = swap(send)
    entering = jnp.where(core == 0, own, got[:PACK])
    mods_own, mods_peer = send[PACK:], got[PACK:]

    def run(entering):
        w_peer, o_peer, cache_peer = swap(w_own), swap(o_own), swap(cache_own)
        x = entering
        mods = [jnp.where(core == t, mods_own, mods_peer) for t in range(2)]
        spread = pl.pallas_call(
            functools.partial(spread_kernel, seq),
            out_shape=shaped(seq, PACK + MODS, LANES),
            in_specs=[VMEM, VMEM],
            out_specs=VMEM,
            compiler_params=params(),
            name="spread",
        )(x, mods[0])
        kept = []
        for t in range(2):
            flags = jnp.stack([(core == t).astype(jnp.int32), core])
            gathered = everyone(spread)
            q, kv = pl.pallas_call(
                functools.partial(project_kernel, seq),
                out_shape=(shaped(HALF, HEAD_DIM), shaped(2, HALF, HEAD_DIM)),
                in_specs=[SMEM, VMEM, ANY, ANY],
                out_specs=(VMEM, VMEM),
                scratch_shapes=[
                    pltpu.VMEM((seq, LANES, 3 * HEAD_DIM), BF16),
                    pltpu.VMEM((seq, REST, 3 * HEAD_DIM), BF16),
                    pltpu.VMEM((HALF, seq * LANES), BF16),
                    pltpu.VMEM((HALF, seq * REST), BF16),
                    pltpu.SemaphoreType.DMA((6,)),
                ],
                compiler_params=params(),
                name="project",
            )(
                flags,
                gathered,
                w_own.reshape(3, seq, width // seq, HEAD_DIM),
                w_peer.reshape(3, seq, width // seq, HEAD_DIM),
            )
            kv_other = swap(kv)
            mixed = pl.pallas_call(
                functools.partial(attend_kernel, seq),
                out_shape=shaped(seq, HALF, HEAD_DIM),
                in_specs=[SMEM, SMEM, VMEM, VMEM, VMEM, VMEM, VMEM],
                out_specs=VMEM,
                compiler_params=params(),
                name="attend",
            )(flags, patch_order, q, kv, kv_other, cache_own, cache_peer)
            heads = everyone(mixed)
            last = t == 1
            results = pl.pallas_call(
                functools.partial(update_kernel, seq, last),
                out_shape=(shaped(PACK, LANES),) + (() if last else (shaped(seq, PACK + MODS, LANES),)),
                in_specs=[SMEM, VMEM, ANY, ANY, VMEM, VMEM] + ([] if last else [VMEM]),
                out_specs=(VMEM,) if last else (VMEM, VMEM),
                scratch_shapes=[
                    pltpu.VMEM(o_own.shape, BF16),
                    pltpu.VMEM((HALF, 2 * LANES), F32),
                    pltpu.SemaphoreType.DMA,
                ],
                compiler_params=params(),
                name="update",
            )(flags, heads, o_own, o_peer, x, mods[t], *([] if last else [mods[1]]))
            x = results[0]
            spread = None if last else results[1]
            kept.append((x, kv, kv_other))
        (x0, kv0, other0), (x1, kv1, other1) = kept
        first = core == 0
        return (
            x1,
            jnp.where(first, x0, x1),
            jnp.where(first, x1, x0),
            jnp.where(first, kv0, kv1),
            jnp.where(first, other0, other1),
        )

    def rest(state):
        return state

    pair = shaped(2, HALF, HEAD_DIM)
    blank = [jnp.zeros(s.shape, s.dtype) for s in (shaped(PACK, LANES), shaped(PACK, LANES), pair, pair)]
    state = lax.cond(second == 0, lambda s: run(s[0]), rest, (entering, *blank))
    arrived = lax.ppermute(state[0], "section", hop_pairs)
    state = lax.cond(second == 1, lambda s: run(s[0]), rest, (arrived, *state[1:]))
    _, mine, theirs, kv, kv_other = state
    other = swap(theirs)
    out_t, cache = pl.pallas_call(
        finish_kernel,
        out_shape=(shaped(SHARD, PATCHES * ROWS), shaped(2, PATCHES * ROWS, HEAD_DIM)),
        in_specs=[SMEM, SMEM, VMEM, VMEM, VMEM, VMEM],
        out_specs=(VMEM, VMEM),
        scratch_shapes=[pltpu.VMEM((PATCHES * ROWS, 2 * LANES), F32)],
        compiler_params=params(),
        name="finish",
    )(core[None], patch_order, mine, other, kv, kv_other)
    return jnp.transpose(out_t, (1, 0))[None], cache[None]


def solution(mesh):
    return jax.shard_map(
        body,
        mesh=mesh,
        in_specs=(
            P("section", None, "seq"),
            P(),
            P(),
            P(None, "section", None, "seq"),
            P("section", None, None, "seq"),
            P("section", None, "seq"),
            P("section", None, None, "seq"),
        ),
        out_specs=(P("section", None, "seq"), P("section", None, None, "seq")),
        check_vma=False,
    )
```

```python
import jax
import jax.numpy as jnp
from jax import lax
from jax.experimental import pallas as pl
from jax.experimental.pallas import tpu as pltpu
from jax.sharding import PartitionSpec as P

HEAD_DIM = 128
PATCHES = 8
CHAIN = 4
EPSILON = 1e-06
ROWS = 64
ALL = PATCHES * ROWS
SIDE = 4
SEQ = SIDE * SIDE
LANES = 128
REST = 64
SHARD = LANES + REST
WIDTH = SEQ * SHARD
PACK = ALL + ALL // 2
MODS = 16
GROUP = PATCHES // SIDE
PART = GROUP * ROWS
WIDE = SIDE * SHARD
HEADS = SIDE * HEAD_DIM
SCALE = HEAD_DIM ** (-0.5)
F32 = jnp.float32
BF16 = jnp.bfloat16
VMEM = pl.BlockSpec(memory_space=pltpu.VMEM)
SMEM = pl.BlockSpec(memory_space=pltpu.SMEM)
ANY = pl.BlockSpec(memory_space=pl.ANY)
ALONG_X = [[SIDE * i + j for i in range(SIDE)] for j in range(SIDE)]
ALONG_Z = [[SIDE * i + j for j in range(SIDE)] for i in range(SIDE)]
TRANSPOSED = (((1,), (1,)), ((), ()))


def shaped(*shape, dtype=BF16):
    return jax.ShapeDtypeStruct(shape, dtype)


def call(kernel, name, out_shape, in_specs, *args, scratch=()):
    many = isinstance(out_shape, tuple)
    return pl.pallas_call(
        kernel,
        out_shape=out_shape,
        in_specs=in_specs,
        out_specs=(VMEM,) * len(out_shape) if many else VMEM,
        scratch_shapes=list(scratch),
        compiler_params=pltpu.CompilerParams(vmem_limit_bytes=32 * 1024 * 1024),
        name=name,
    )(*args)


def low_lanes(rows):
    return lax.broadcasted_iota(jnp.int32, (rows, LANES), 1) < REST


def patch_at(order_ref, j, base=0):
    return pl.ds(pl.multiple_of(base + order_ref[j] * ROWS, ROWS), ROWS)


def tile(k):
    return slice(k * LANES, (k + 1) * LANES)


def pair_lanes(low, even, odd):
    return jnp.where(low, even, pltpu.roll(odd, REST, 1))


def softmax_mix(q, keys, values):
    scores = lax.dot_general(q, keys, TRANSPOSED, preferred_element_type=F32) * SCALE
    terms = jnp.exp(scores - jnp.max(scores, axis=1, keepdims=True))
    weights = (terms / jnp.sum(terms, axis=1, keepdims=True)).astype(BF16)
    return jnp.dot(weights, values, preferred_element_type=F32).astype(BF16)


def pack_kernel(order_ref, lat_ref, mod_ref, out_ref, rows_ref):
    rows_ref[:, :SHARD] = lat_ref[...].astype(F32).T
    low = low_lanes(ROWS)
    rest = []
    for j in range(PATCHES):
        at = patch_at(order_ref, j)
        out_ref[j * ROWS : (j + 1) * ROWS, :] = rows_ref[at, :LANES].astype(BF16)
        rest.append(rows_ref[at, LANES:])
    half = PATCHES // 2
    for j in range(half):
        both = pair_lanes(low, rest[j], rest[j + half])
        out_ref[ALL + j * ROWS : ALL + (j + 1) * ROWS, :] = both.astype(BF16)
    mod = mod_ref[...]
    lines = []
    for kind in (1.0 + mod[1:2], mod[0:1], mod[2:3]):
        last = jnp.concatenate([kind[:, LANES:], kind[:, LANES:]], axis=1)
        for value in (kind[:, :LANES], last):
            high = value.astype(BF16).astype(F32)
            lines += [high, value - high]
    lines.append(jnp.zeros((MODS - len(lines), LANES), F32))
    out_ref[PACK:, :] = jnp.concatenate(lines, axis=0).astype(BF16)


def repeat_kernel(in_ref, out_ref):
    for s in range(SIDE):
        out_ref[s] = in_ref[...]


def project_whole_kernel(x_ref, w_ref, q_ref, kv_ref, wm_ref, wr_ref, nm_ref, nr_ref, sems):
    copies = []
    for t in range(3):
        lanes = pl.ds(t * HEAD_DIM, HEAD_DIM)
        copies.append(pltpu.make_async_copy(w_ref.at[t, :, :LANES, :], wm_ref.at[:, :, lanes], sems.at[2 * t]))
        copies.append(pltpu.make_async_copy(w_ref.at[t, :, LANES:, :], wr_ref.at[:, :, lanes], sems.at[2 * t + 1]))
    for copy in copies:
        copy.start()
    low = low_lanes(ROWS)

    def line(s, k):
        rows = x_ref[s, PACK:, :].astype(F32)
        return rows[2 * k : 2 * k + 1] + rows[2 * k + 1 : 2 * k + 2]

    scale_first = [line(s, 0) for s in range(SEQ)]
    shift_first = [line(s, 2) for s in range(SEQ)]
    scale_last = [jnp.where(low[:1], line(2 * p, 1), line(2 * p + 1, 1)) for p in range(SEQ // 2)]
    shift_last = [jnp.where(low[:1], line(2 * p, 3), line(2 * p + 1, 3)) for p in range(SEQ // 2)]
    half = PATCHES // 2
    for j in range(PATCHES):
        mine = pl.ds(j * ROWS, ROWS)
        rest = pl.ds(ALL + (j % half) * ROWS, ROWS)
        total, square, total_rest, square_rest = (jnp.zeros((ROWS, LANES), F32) for _ in range(4))
        for s in range(SEQ):
            x = x_ref[s, mine, :].astype(F32)
            total = total + x
            square = square + x * x
            x = x_ref[s, rest, :].astype(F32)
            total_rest = total_rest + x
            square_rest = square_rest + x * x
        in_half = low if j < half else jnp.logical_not(low)
        total = total + jnp.where(in_half, total_rest, 0.0)
        square = square + jnp.where(in_half, square_rest, 0.0)
        mean = jnp.sum(total, axis=1, keepdims=True) / WIDTH
        var = jnp.sum(square, axis=1, keepdims=True) / WIDTH - mean * mean
        rstd = lax.rsqrt(var + EPSILON)
        for s in range(SEQ):
            x = x_ref[s, mine, :].astype(F32)
            nm_ref[mine, tile(s)] = ((x - mean) * rstd * scale_first[s] + shift_first[s]).astype(BF16)
        for p in range(SEQ // 2):
            even = x_ref[2 * p, rest, :].astype(F32)
            odd = x_ref[2 * p + 1, rest, :].astype(F32)
            if j < half:
                x = pair_lanes(low, even, odd)
            else:
                x = jnp.where(low, pltpu.roll(even, REST, 1), odd)
            nr_ref[mine, tile(p)] = ((x - mean) * rstd * scale_last[p] + shift_last[p]).astype(BF16)
    for copy in copies:
        copy.wait()
    qkv = jnp.dot(nm_ref[...], wm_ref[...].reshape(SEQ * LANES, 3 * HEAD_DIM), preferred_element_type=F32)
    qkv = qkv + jnp.dot(nr_ref[...], wr_ref[...].reshape(SEQ * REST, 3 * HEAD_DIM), preferred_element_type=F32)
    qkv = qkv.astype(BF16)
    q_ref[...] = qkv[:, :HEAD_DIM]
    kv_ref[0] = qkv[:, HEAD_DIM : 2 * HEAD_DIM]
    kv_ref[1] = qkv[:, 2 * HEAD_DIM :]


def attend_whole_kernel(order_ref, q_ref, kv_ref, stale_ref, out_ref):
    stale = [[stale_ref[part, patch_at(order_ref, j), :] for j in range(PATCHES)] for part in range(2)]
    for j in range(PATCHES):
        at = slice(j * ROWS, (j + 1) * ROWS)
        keys, values = (
            jnp.concatenate([kv_ref[part, : (j + 1) * ROWS, :]] + stale[part][j + 1 :], axis=0) for part in range(2)
        )
        mixed = softmax_mix(q_ref[at, :], keys, values)
        for s in range(SIDE):
            out_ref[s, at, :] = mixed


def update_whole_kernel(mixed_ref, w_ref, x_ref, out_ref, held_ref):
    mixed = jnp.concatenate([mixed_ref[h // SIDE, h % SIDE] for h in range(SEQ)], axis=1)
    held_ref[:, :SHARD] = lax.dot_general(mixed, w_ref[...], TRANSPOSED, preferred_element_type=F32)
    mods = x_ref[PACK:, :].astype(F32)
    gate_first = mods[8:9] + mods[9:10]
    gate_last = mods[10:11] + mods[11:12]
    half = ALL // 2
    for i in range(SIDE):
        at = slice(i * PART, (i + 1) * PART)
        out_ref[i, :, :LANES] = (x_ref[at, :].astype(F32) + gate_first * held_ref[at, :LANES]).astype(BF16)
        rest = x_ref[ALL + (i * PART) % half : ALL + (i * PART) % half + PART, :].astype(F32)
        if i >= SIDE // 2:
            rest = pltpu.roll(rest, REST, 1)
        rest = rest + gate_last * held_ref[at, LANES:]
        out_ref[i, :, LANES:] = jnp.where(low_lanes(PART), rest, 0.0).astype(BF16)


def join_kernel(in_ref, out_ref):
    low = low_lanes(PART)
    for i in range(SIDE):
        out_ref[:, tile(i)] = in_ref[i, :, :LANES]
    for m in range(SIDE // 2):
        even, odd = (in_ref[2 * m + k, :, LANES:].astype(F32) for k in range(2))
        out_ref[:, tile(SIDE + m)] = pair_lanes(low, even, odd).astype(BF16)


def part_kernel(in_ref, out_ref):
    low = low_lanes(PART)
    for i in range(SIDE):
        rest = in_ref[:, tile(SIDE + i // 2)].astype(F32)
        if i % 2:
            rest = pltpu.roll(rest, REST, 1)
        out_ref[i, :, :LANES] = in_ref[:, tile(i)]
        out_ref[i, :, LANES:] = jnp.where(low, rest, 0.0).astype(BF16)


def mods_kernel(gathered_ref, out_ref):
    low = low_lanes(1)
    rows = [gathered_ref[i, 2 * ALL :, :].astype(F32) for i in range(SIDE)]
    lines = []
    for k in range(3):
        for h in range(2):
            first, last = 4 * k + h, 4 * k + 2 + h
            parts = [rows[i][first : first + 1] for i in range(SIDE)]
            for m in range(SIDE // 2):
                even, odd = (rows[2 * m + e][last : last + 1] for e in range(2))
                parts.append(jnp.where(low, even, odd))
            lines.append(jnp.concatenate(parts, axis=1))
    lines.append(jnp.zeros((MODS - len(lines), WIDE), F32))
    out_ref[...] = jnp.concatenate(lines, axis=0).astype(BF16)


def spread_kernel(x_ref, mods_ref, out_ref):
    for s in range(SIDE):
        out_ref[s, :PART, :] = x_ref[...]
        out_ref[s, PART:, :] = mods_ref[...]


def project_kernel(x_ref, w_ref, q_ref, kv_ref, wm_ref, wr_ref, nm_ref, nr_ref, sems):
    copies = []
    for t in range(3):
        for h in range(SIDE):
            lanes = pl.ds((t * SIDE + h) * HEAD_DIM, HEAD_DIM)
            pairs = [(w_ref.at[h, t, :, :, :LANES, :], wm_ref.at[:, :, :, lanes])]
            pairs += [(w_ref.at[h, t, :, j, LANES:, :], wr_ref.at[j, :, :, lanes]) for j in range(SIDE)]
            copies += [pltpu.make_async_copy(a, b, sems.at[len(copies) + n]) for n, (a, b) in enumerate(pairs)]
    for copy in copies:
        copy.start()
    mods = [x_ref[j, PART:, :].astype(F32) for j in range(SIDE)]
    scale = [m[0:1] + m[1:2] for m in mods]
    shift = [m[2:3] + m[3:4] for m in mods]
    tiles = WIDE // LANES
    for g in range(GROUP):
        mine = pl.ds(g * ROWS, ROWS)
        total, square = (jnp.zeros((ROWS, LANES), F32) for _ in range(2))
        for j in range(SIDE):
            for k in range(tiles):
                x = x_ref[j, mine, tile(k)].astype(F32)
                total = total + x
                square = square + x * x
        mean = jnp.sum(total, axis=1, keepdims=True) / WIDTH
        var = jnp.sum(square, axis=1, keepdims=True) / WIDTH - mean * mean
        rstd = lax.rsqrt(var + EPSILON)
        for j in range(SIDE):
            for k in range(tiles):
                x = x_ref[j, mine, tile(k)].astype(F32)
                normed = ((x - mean) * rstd * scale[j][:, tile(k)] + shift[j][:, tile(k)]).astype(BF16)
                if k < SIDE:
                    nm_ref[mine, tile(k * SIDE + j)] = normed
                else:
                    nr_ref[mine, tile(j * (SIDE // 2) + k - SIDE)] = normed
    each = len(copies) // 3
    for t in range(3):
        for copy in copies[t * each : (t + 1) * each]:
            copy.wait()
        lanes = slice(t * HEADS, (t + 1) * HEADS)
        part = jnp.dot(nm_ref[...], wm_ref[:, :, :, lanes].reshape(SEQ * LANES, HEADS), preferred_element_type=F32)
        part = part + jnp.dot(nr_ref[...], wr_ref[:, :, :, lanes].reshape(SEQ * REST, HEADS), preferred_element_type=F32)
        part = part.astype(BF16)
        if t == 0:
            q_ref[...] = part
        else:
            for s in range(SIDE):
                kv_ref[s, :, (t - 1) * HEADS : t * HEADS] = part


def attend_kernel(row_ref, order_ref, q_ref, kv_ref, stale_ref, out_ref, own_ref):
    i = row_ref[0]
    for h in range(SIDE):
        new, old = [], []
        for part in range(2):
            lanes = tile(part * SIDE + h)
            new.append([kv_ref[n // GROUP, (n % GROUP) * ROWS : (n % GROUP + 1) * ROWS, lanes] for n in range(PATCHES)])
            old.append([stale_ref[h, patch_at(order_ref, n, part * ALL), :] for n in range(PATCHES)])
        for g in range(GROUP):
            at = slice(g * ROWS, (g + 1) * ROWS)
            keys, values = (
                jnp.concatenate(
                    [jnp.where(n <= GROUP * i + g, new[part][n], old[part][n]) for n in range(PATCHES)], axis=0
                )
                for part in range(2)
            )
            mixed = softmax_mix(q_ref[at, tile(h)], keys, values)
            for s in range(SIDE):
                out_ref[s, at, tile(h)] = mixed
    for part in range(2):
        lanes = pl.ds(pl.multiple_of(part * HEADS + i * HEAD_DIM, HEAD_DIM), HEAD_DIM)
        for n in range(SIDE):
            own_ref[part, n * PART : (n + 1) * PART, :] = kv_ref[n, :, lanes]


def update_kernel(mixed_ref, w_ref, x_ref, mods_ref, out_ref, held_ref, sems):
    copies = []
    for i in range(SIDE):
        first = held_ref.at[i * LANES : (i + 1) * LANES, :]
        last = held_ref.at[SIDE * LANES + i * REST : SIDE * LANES + (i + 1) * REST, :]
        copies.append(pltpu.make_async_copy(w_ref.at[i, :LANES, :], first, sems.at[2 * i]))
        copies.append(pltpu.make_async_copy(w_ref.at[i, LANES:, :], last, sems.at[2 * i + 1]))
    for copy in copies:
        copy.start()
    mixed = jnp.concatenate([mixed_ref[h % SIDE, :, tile(h // SIDE)] for h in range(SEQ)], axis=1)
    for copy in copies:
        copy.wait()
    made = lax.dot_general(mixed, held_ref[...], TRANSPOSED, preferred_element_type=F32)
    mods = mods_ref[...].astype(F32)
    out_ref[...] = (x_ref[...].astype(F32) + (mods[4:5] + mods[5:6]) * made).astype(BF16)


def finish_kernel(order_ref, x_ref, kv_ref, out_ref, cache_ref, rows_ref):
    for j in range(PATCHES):
        at = patch_at(order_ref, j)
        rows_ref[at, :] = x_ref[j // GROUP, (j % GROUP) * ROWS : (j % GROUP + 1) * ROWS, :].astype(F32)
        for part in range(2):
            cache_ref[part, at, :] = kv_ref[part, j * ROWS : (j + 1) * ROWS, :]
    out_ref[...] = rows_ref[...].T[:SHARD, :].astype(BF16)


def blank(*shapes):
    return pl.pallas_call(lambda *refs: None, out_shape=shapes, out_specs=(ANY,) * len(shapes), name="blank")()


def body(latents, patch_order, timestep, mod_table, w_qkv, w_out, kv_cache):
    sections = lax.axis_size("section")
    position = lax.axis_index("section") % CHAIN
    row = (lax.axis_index("seq") // SIDE).astype(jnp.int32)[None]
    w_own = jnp.transpose(w_qkv[0], (1, 0, 2))
    o_own = jnp.transpose(w_out[0], (1, 0))
    cache_own = kv_cache[0]
    mod_now = lax.dynamic_index_in_dim(mod_table, timestep[0], 0, keepdims=False)[0]

    def exchange(value, groups):
        return lax.all_to_all(value, "seq", 0, 0, axis_index_groups=groups)

    def gather(value, groups):
        return exchange(jnp.broadcast_to(value[None], (SIDE,) + value.shape), groups)

    packed = call(
        pack_kernel,
        "pack",
        shaped(PACK + MODS, LANES),
        [SMEM, VMEM, VMEM],
        patch_order,
        jnp.transpose(latents[0], (1, 0)),
        mod_now,
        scratch=[pltpu.VMEM((ALL, 2 * LANES), F32)],
    )
    rows_shape, kv_shape, x_shape = shaped(SIDE, PART, 2 * LANES), shaped(2, ALL, HEAD_DIM), shaped(PART, WIDE)

    def first_block(packed):
        gathered = gather(gather(packed, ALONG_Z), ALONG_X).reshape(SEQ, PACK + MODS, LANES)
        q, kv = call(
            project_whole_kernel,
            "project_whole",
            (shaped(ALL, HEAD_DIM), kv_shape),
            [VMEM, ANY],
            gathered,
            w_own.reshape(3, SEQ, SHARD, HEAD_DIM),
            scratch=[
                pltpu.VMEM((SEQ, LANES, 3 * HEAD_DIM), BF16),
                pltpu.VMEM((SEQ, REST, 3 * HEAD_DIM), BF16),
                pltpu.VMEM((ALL, SEQ * LANES), BF16),
                pltpu.VMEM((ALL, SEQ * REST), BF16),
                pltpu.SemaphoreType.DMA((6,)),
            ],
        )
        mixed = call(
            attend_whole_kernel,
            "attend_whole",
            shaped(SIDE, ALL, HEAD_DIM),
            [SMEM, VMEM, VMEM, VMEM],
            patch_order,
            q,
            kv,
            cache_own,
        )
        heads = gather(exchange(mixed, ALONG_Z), ALONG_X)
        rows = call(
            update_whole_kernel,
            "update_whole",
            rows_shape,
            [VMEM, VMEM, VMEM],
            heads,
            o_own,
            packed,
            scratch=[pltpu.VMEM((ALL, 2 * LANES), F32)],
        )
        x = call(join_kernel, "join", x_shape, [VMEM], exchange(rows, ALONG_X))
        return x, rows, kv

    def prepare(packed):
        w = gather(w_own, ALONG_X).reshape(SIDE, 3, SIDE, SIDE, SHARD, HEAD_DIM)
        o = gather(o_own, ALONG_X)
        small = jnp.concatenate([cache_own.reshape(2 * ALL, HEAD_DIM), packed[PACK:]], axis=0)
        small = gather(small, ALONG_X)
        mods = call(mods_kernel, "mods", shaped(MODS, WIDE), [VMEM], small)
        return w, o, small, mods

    def later_block(x, w, o, small, mods):
        spread = call(spread_kernel, "spread", shaped(SIDE, PART + MODS, WIDE), [VMEM, VMEM], x, mods)
        q, kv = call(
            project_kernel,
            "project",
            (shaped(PART, HEADS), shaped(SIDE, PART, 2 * HEADS)),
            [VMEM, ANY],
            exchange(spread, ALONG_Z),
            w,
            scratch=[
                pltpu.VMEM((SIDE, SIDE, LANES, 3 * HEADS), BF16),
                pltpu.VMEM((SIDE, SIDE, REST, 3 * HEADS), BF16),
                pltpu.VMEM((PART, SEQ * LANES), BF16),
                pltpu.VMEM((PART, SEQ * REST), BF16),
                pltpu.SemaphoreType.DMA((60,)),
            ],
        )
        mixed, kv_own = call(
            attend_kernel,
            "attend",
            (shaped(SIDE, PART, HEADS), kv_shape),
            [SMEM, SMEM, VMEM, VMEM, VMEM],
            row,
            patch_order,
            q,
            exchange(kv, ALONG_X),
            small,
        )
        new = call(
            update_kernel,
            "update",
            x_shape,
            [VMEM, ANY, VMEM, VMEM],
            exchange(mixed, ALONG_Z),
            o,
            x,
            mods,
            scratch=[pltpu.VMEM((WIDE, SEQ * HEAD_DIM), BF16), pltpu.SemaphoreType.DMA((2 * SIDE,))],
        )
        return new, kv_own

    def nothing_yet(packed):
        return tuple(jnp.zeros(s.shape, s.dtype) for s in (x_shape, rows_shape, kv_shape))

    def no_weights(packed):
        return blank(
            shaped(SIDE, 3, SIDE, SIDE, SHARD, HEAD_DIM),
            shaped(SIDE, SHARD, SEQ * HEAD_DIM),
            shaped(SIDE, 2 * ALL + MODS, LANES),
            shaped(MODS, WIDE),
        )

    x, rows, kv = lax.cond(position == 0, first_block, nothing_yet, packed)
    weights = lax.cond(position > 0, prepare, no_weights, packed)
    (x, weights) = lax.optimization_barrier((x, weights))
    for p in range(1, CHAIN):
        pairs = [(s, s + 1) for s in range(sections) if s % CHAIN == p - 1]
        arrived = lax.ppermute(x, "section", pairs)
        x, kv = lax.cond(
            position == p,
            lambda arrived, x, kv, *weights: later_block(arrived, *weights),
            lambda arrived, x, kv, *weights: (x, kv),
            arrived,
            x,
            kv,
            *weights,
        )
    rows = lax.cond(
        position > 0,
        lambda x, rows: exchange(call(part_kernel, "part", rows_shape, [VMEM], x), ALONG_X),
        lambda x, rows: rows,
        x,
        rows,
    )
    out_t, cache = call(
        finish_kernel,
        "finish",
        (shaped(SHARD, ALL), kv_shape),
        [SMEM, VMEM, VMEM],
        patch_order,
        rows,
        kv,
        scratch=[pltpu.VMEM((ALL, 2 * LANES), F32)],
    )
    return jnp.transpose(out_t, (1, 0))[None], cache[None]


def solution(mesh):
    return jax.shard_map(
        body,
        mesh=mesh,
        in_specs=(
            P("section", None, "seq"),
            P(),
            P(),
            P(None, "section", None, "seq"),
            P("section", None, None, "seq"),
            P("section", None, "seq"),
            P("section", None, None, "seq"),
        ),
        out_specs=(P("section", None, "seq"), P("section", None, None, "seq")),
        check_vma=False,
    )
```

```python
import functools

import jax
import jax.numpy as jnp
from jax import lax
from jax.experimental import pallas as pl
from jax.experimental.pallas import tpu as pltpu
from jax.sharding import PartitionSpec as P

HEAD_DIM = 128
PATCHES = 8
CHAIN = 4
EPSILON = 1e-06
ROWS = 64
ALL = PATCHES * ROWS
SIDE = 4
SEQ = SIDE * SIDE
LANES = 128
REST = 64
SHARD = LANES + REST
WIDTH = SEQ * SHARD
HALF = ALL // 2
QUARTER = HALF // 2
PACK = HALF + QUARTER
MODS = 16
CACHE = PACK + MODS
GROUP = PATCHES // SIDE
PART = GROUP * ROWS
WIDE = SIDE * SHARD
HEADS = SIDE * HEAD_DIM
SCALE = HEAD_DIM ** (-0.5)
F32 = jnp.float32
BF16 = jnp.bfloat16
VMEM = pl.BlockSpec(memory_space=pltpu.VMEM)
SMEM = pl.BlockSpec(memory_space=pltpu.SMEM)
ANY = pl.BlockSpec(memory_space=pl.ANY)
ALONG_X = [[SIDE * i + j for i in range(SIDE)] for j in range(SIDE)]
ALONG_Z = [[SIDE * i + j for j in range(SIDE)] for i in range(SIDE)]
TRANSPOSED = (((1,), (1,)), ((), ()))


def shaped(*shape, dtype=BF16):
    return jax.ShapeDtypeStruct(shape, dtype)


def call(kernel, name, out_shape, in_specs, *args, scratch=(), mib=12):
    many = isinstance(out_shape, tuple)
    return pl.pallas_call(
        kernel,
        out_shape=out_shape,
        in_specs=in_specs,
        out_specs=(VMEM,) * len(out_shape) if many else VMEM,
        scratch_shapes=list(scratch),
        compiler_params=pltpu.CompilerParams(vmem_limit_bytes=mib * 1024 * 1024),
        name=name,
    )(*args)


def low_lanes(rows):
    return lax.broadcasted_iota(jnp.int32, (rows, LANES), 1) < REST


def patch_at(order_ref, j, base=0):
    return pl.ds(pl.multiple_of(base + order_ref[j] * ROWS, ROWS), ROWS)


def tile(k):
    return slice(k * LANES, (k + 1) * LANES)


def pair_lanes(low, even, odd):
    return jnp.where(low, even, pltpu.roll(odd, REST, 1))


def softmax_mix(queries, keys, values):
    scores = [
        lax.dot_general(q, k, TRANSPOSED, preferred_element_type=F32) * SCALE for q, k in zip(queries, keys, strict=True)
    ]
    tops = [jnp.max(x, axis=1, keepdims=True) for x in scores]
    terms = [jnp.exp(x - top) for x, top in zip(scores, tops, strict=True)]
    sums = [jnp.sum(x, axis=1, keepdims=True) for x in terms]
    weights = [(x * (1.0 / total)).astype(BF16) for x, total in zip(terms, sums, strict=True)]
    return [jnp.dot(w, v, preferred_element_type=F32).astype(BF16) for w, v in zip(weights, values, strict=True)]


def pack_kernel(order_ref, lat_ref, mod_ref, cache_ref, own_ref, send_ref, rows_ref):
    rows_ref[:, :SHARD] = lat_ref[...].astype(F32).T
    low = low_lanes(ROWS)
    for core, out_ref in ((0, own_ref), (1, send_ref)):
        rest = []
        for j in range(SIDE):
            at = patch_at(order_ref, core * SIDE + j)
            out_ref[j * ROWS : (j + 1) * ROWS, :] = rows_ref[at, :LANES].astype(BF16)
            rest.append(rows_ref[at, LANES:])
        for j in range(2):
            both = pair_lanes(low, rest[j], rest[j + 2])
            out_ref[HALF + j * ROWS : HALF + (j + 1) * ROWS, :] = both.astype(BF16)
    mod = mod_ref[...]
    lines = []
    for kind in (1.0 + mod[1:2], mod[0:1], mod[2:3]):
        last = jnp.concatenate([kind[:, LANES:], kind[:, LANES:]], axis=1)
        for value in (kind[:, :LANES], last):
            high = value.astype(BF16).astype(F32)
            lines += [high, value - high]
    lines.append(jnp.zeros((MODS - len(lines), LANES), F32))
    send_ref[PACK : PACK + MODS, :] = jnp.concatenate(lines, axis=0).astype(BF16)
    for part in range(2):
        send_ref[CACHE + part * ALL : CACHE + (part + 1) * ALL, :] = cache_ref[part]


def mods_of(flag_ref, t, send_ref, got_ref):
    return jnp.where(flag_ref[t] == 1, send_ref[PACK:CACHE, :], got_ref[PACK:CACHE, :])


def start_kernel(flag_ref, own_ref, send_ref, got_ref, x_ref, out_ref):
    x = jnp.where(flag_ref[2] == 0, own_ref[...], got_ref[:PACK, :])
    mods = mods_of(flag_ref, 0, send_ref, got_ref)
    x_ref[...] = x
    for s in range(SIDE):
        out_ref[s, :PACK, :] = x
        out_ref[s, PACK:, :] = mods


def place(flag_ref, s):
    return jnp.where(flag_ref[2] == 0, s, (s % SIDE) * SIDE + s // SIDE)


def project_half_kernel(t_now, flag_ref, x_ref, own_ref, peer_ref, q_ref, kv_ref, wm_ref, wr_ref, nm_ref, nr_ref, sems):
    def copies(w_ref):
        found = []
        for t in range(3):
            lanes = pl.ds(t * HEAD_DIM, HEAD_DIM)
            found.append(pltpu.make_async_copy(w_ref.at[t, :, :LANES, :], wm_ref.at[:, :, lanes], sems.at[2 * t]))
            found.append(pltpu.make_async_copy(w_ref.at[t, :, LANES:, :], wr_ref.at[:, :, lanes], sems.at[2 * t + 1]))
        return found

    @pl.when(flag_ref[t_now] == 1)
    def _():
        for copy in copies(own_ref):
            copy.start()

    @pl.when(flag_ref[t_now] == 0)
    def _():
        for copy in copies(peer_ref):
            copy.start()

    low = low_lanes(ROWS)
    at = [place(flag_ref, s) for s in range(SEQ)]

    def line(s, k):
        pair = x_ref[at[s], PACK:, :].astype(F32)
        return pair[2 * k : 2 * k + 1] + pair[2 * k + 1 : 2 * k + 2]

    scale_first = [line(s, 0) for s in range(SEQ)]
    shift_first = [line(s, 2) for s in range(SEQ)]
    scale_last = [jnp.where(low[:1], line(2 * p, 1), line(2 * p + 1, 1)) for p in range(SEQ // 2)]
    shift_last = [jnp.where(low[:1], line(2 * p, 3), line(2 * p + 1, 3)) for p in range(SEQ // 2)]
    for j in range(SIDE):
        mine = pl.ds(j * ROWS, ROWS)
        rest = pl.ds(HALF + (j % 2) * ROWS, ROWS)
        total = jnp.zeros((ROWS, LANES), F32)
        square = jnp.zeros((ROWS, LANES), F32)
        total_rest = jnp.zeros((ROWS, LANES), F32)
        square_rest = jnp.zeros((ROWS, LANES), F32)
        for s in range(SEQ):
            x = x_ref[at[s], mine, :].astype(F32)
            total = total + x
            square = square + x * x
            x = x_ref[at[s], rest, :].astype(F32)
            total_rest = total_rest + x
            square_rest = square_rest + x * x
        in_half = low if j < 2 else jnp.logical_not(low)
        total = total + jnp.where(in_half, total_rest, 0.0)
        square = square + jnp.where(in_half, square_rest, 0.0)
        mean = jnp.sum(total, axis=1, keepdims=True) / WIDTH
        var = jnp.sum(square, axis=1, keepdims=True) / WIDTH - mean * mean
        rstd = lax.rsqrt(var + EPSILON)
        for s in range(SEQ):
            x = x_ref[at[s], mine, :].astype(F32)
            normed = (x - mean) * rstd * scale_first[s] + shift_first[s]
            nm_ref[mine, tile(s)] = normed.astype(BF16)
        for p in range(SEQ // 2):
            even = x_ref[at[2 * p], rest, :].astype(F32)
            odd = x_ref[at[2 * p + 1], rest, :].astype(F32)
            if j < 2:
                x = pair_lanes(low, even, odd)
            else:
                x = jnp.where(low, pltpu.roll(even, REST, 1), odd)
            normed = (x - mean) * rstd * scale_last[p] + shift_last[p]
            nr_ref[mine, tile(p)] = normed.astype(BF16)

    for copy in copies(own_ref):
        copy.wait()
    w_first = wm_ref[...].reshape(SEQ * LANES, 3 * HEAD_DIM)
    w_last = wr_ref[...].reshape(SEQ * REST, 3 * HEAD_DIM)
    qkv = jnp.dot(nm_ref[...], w_first, preferred_element_type=F32)
    qkv = qkv + jnp.dot(nr_ref[...], w_last, preferred_element_type=F32)
    qkv = qkv.astype(BF16)
    q_ref[...] = qkv[:, :HEAD_DIM]
    kv_ref[0] = qkv[:, HEAD_DIM : 2 * HEAD_DIM]
    kv_ref[1] = qkv[:, 2 * HEAD_DIM :]


def attend_half_kernel(t, flag_ref, order_ref, q_ref, kv_ref, other_ref, own_ref, got_ref, out_ref):
    mine = flag_ref[t] == 1
    core = flag_ref[2]

    def stale(part, j):
        peer = got_ref[patch_at(order_ref, j, CACHE + part * ALL), :]
        return jnp.where(mine, own_ref[part, patch_at(order_ref, j), :], peer)

    old, other = [], []
    for part in range(2):
        old.append([stale(part, core * SIDE + j) for j in range(SIDE)])
        kept = jnp.concatenate([stale(part, (1 - core) * SIDE + j) for j in range(SIDE)], axis=0)
        other.append(jnp.where(core == 1, other_ref[part], kept))
    queries, keys, values = [], [], []
    for j in range(SIDE):
        queries.append(q_ref[j * ROWS : (j + 1) * ROWS, :])
        for part, found in ((0, keys), (1, values)):
            parts = [kv_ref[part, : (j + 1) * ROWS, :]] + old[part][j + 1 :] + [other[part]]
            found.append(jnp.concatenate(parts, axis=0))
    for j, mixed in enumerate(softmax_mix(queries, keys, values)):
        for s in range(SIDE):
            out_ref[s, j * ROWS : (j + 1) * ROWS, :] = mixed


def update_half_kernel(t, flag_ref, mixed_ref, own_ref, peer_ref, x_ref, send_ref, got_ref, rows_ref, *refs):
    last = t == 1
    if last:
        w_ref, held_ref, sem = refs
    else:
        new_ref, spread_ref, w_ref, held_ref, sem = refs

    @pl.when(flag_ref[t] == 1)
    def _():
        pltpu.make_async_copy(own_ref, w_ref, sem).start()

    @pl.when(flag_ref[t] == 0)
    def _():
        pltpu.make_async_copy(peer_ref, w_ref, sem).start()

    mixed = jnp.concatenate([mixed_ref[place(flag_ref, h)] for h in range(SEQ)], axis=1)
    pltpu.make_async_copy(own_ref, w_ref, sem).wait()
    held_ref[:, :SHARD] = lax.dot_general(mixed, w_ref[...], TRANSPOSED, preferred_element_type=F32)
    mods = mods_of(flag_ref, t, send_ref, got_ref).astype(F32)
    gate_first = mods[8:9] + mods[9:10]
    gate_last = mods[10:11] + mods[11:12]
    first = (x_ref[:HALF, :].astype(F32) + gate_first * held_ref[:, :LANES]).astype(BF16)
    made = pair_lanes(low_lanes(QUARTER), held_ref[:QUARTER, LANES:], held_ref[QUARTER:, LANES:])
    rest = x_ref[HALF:, :].astype(F32) + gate_last * made
    other = pltpu.roll(rest, REST, 1).astype(BF16)
    rest = rest.astype(BF16)
    for n in range(SIDE):
        at = slice((n % 2) * ROWS, (n % 2 + 1) * ROWS)
        rows_ref[n, :, :LANES] = first[n * ROWS : (n + 1) * ROWS]
        rows_ref[n, :, LANES:] = rest[at] if n < 2 else other[at]
    if not last:
        mods = mods_of(flag_ref, 1, send_ref, got_ref)
        new_ref[:HALF, :] = first
        new_ref[HALF:, :] = rest
        for s in range(SIDE):
            spread_ref[s, :HALF, :] = first
            spread_ref[s, HALF:PACK, :] = rest
            spread_ref[s, PACK:, :] = mods


def join_kernel(in_ref, out_ref):
    low = low_lanes(ROWS)
    for i in range(SIDE):
        out_ref[:, tile(i)] = in_ref[i, :, :LANES]
    for m in range(SIDE // 2):
        even, odd = (in_ref[2 * m + k, :, LANES:].astype(F32) for k in range(2))
        out_ref[:, tile(SIDE + m)] = pair_lanes(low, even, odd).astype(BF16)


def mods_kernel(gathered_ref, out_ref):
    low = low_lanes(1)
    rows = [gathered_ref[i, :MODS, :].astype(F32) for i in range(SIDE)]
    lines = []
    for k in range(3):
        for h in range(2):
            first, last = 4 * k + h, 4 * k + 2 + h
            parts = [rows[i][first : first + 1] for i in range(SIDE)]
            for m in range(SIDE // 2):
                even, odd = (rows[2 * m + e][last : last + 1] for e in range(2))
                parts.append(jnp.where(low, even, odd))
            lines.append(jnp.concatenate(parts, axis=1))
    lines.append(jnp.zeros((MODS - len(lines), WIDE), F32))
    out_ref[...] = jnp.concatenate(lines, axis=0).astype(BF16)


def spread_kernel(low_ref, high_ref, x_ref, out_ref):
    x_ref[:ROWS, :] = low_ref[...]
    x_ref[ROWS:, :] = high_ref[...]
    for s in range(SIDE):
        out_ref[s, :ROWS, :] = low_ref[...]
        out_ref[s, ROWS:, :] = high_ref[...]


def project_kernel(row_ref, x_ref, mods_ref, w_ref, below_ref, above_ref, *refs):
    across_low_ref, across_high_ref, q_ref, kv_ref, wm_ref, wr_ref, nm_ref, nr_ref, sems = refs
    i = row_ref[0]
    half = SIDE // 2
    sources = (
        (w_ref, 0, SIDE, i),
        (below_ref, 0, SIDE, lax.rem(i + 3, SIDE)),
        (above_ref, 0, SIDE, lax.rem(i + 1, SIDE)),
        (across_low_ref, 0, half, lax.rem(i + 2, SIDE)),
        (across_high_ref, half, SIDE, lax.rem(i + 2, SIDE)),
    )
    copies = []
    for t in range(3):
        for source, first, last, h in sources:
            lanes = pl.ds(pl.multiple_of((t * SIDE + h) * HEAD_DIM, HEAD_DIM), HEAD_DIM)
            pairs = [(source.at[t, :, :, :LANES, :], wm_ref.at[first:last, :, :, lanes])]
            pairs += [(source.at[t, :, j, LANES:, :], wr_ref.at[j, first:last, :, lanes]) for j in range(SIDE)]
            copies += [pltpu.make_async_copy(a, b, sems.at[len(copies) + n]) for n, (a, b) in enumerate(pairs)]
    for copy in copies:
        copy.start()
    mods = [mods_ref[j].astype(F32) for j in range(SIDE)]
    scale = [m[0:1] + m[1:2] for m in mods]
    shift = [m[2:3] + m[3:4] for m in mods]
    tiles = WIDE // LANES
    for g in range(GROUP):
        mine = pl.ds(g * ROWS, ROWS)
        total, square = (jnp.zeros((ROWS, LANES), F32) for _ in range(2))
        for j in range(SIDE):
            for k in range(tiles):
                x = x_ref[j, mine, tile(k)].astype(F32)
                total = total + x
                square = square + x * x
        mean = jnp.sum(total, axis=1, keepdims=True) / WIDTH
        var = jnp.sum(square, axis=1, keepdims=True) / WIDTH - mean * mean
        rstd = lax.rsqrt(var + EPSILON)
        for j in range(SIDE):
            for k in range(tiles):
                x = x_ref[j, mine, tile(k)].astype(F32)
                normed = ((x - mean) * rstd * scale[j][:, tile(k)] + shift[j][:, tile(k)]).astype(BF16)
                if k < SIDE:
                    nm_ref[mine, tile(k * SIDE + j)] = normed
                else:
                    nr_ref[mine, tile(j * (SIDE // 2) + k - SIDE)] = normed
    each = len(copies) // 3
    for t in range(3):
        for copy in copies[t * each : (t + 1) * each]:
            copy.wait()
        lanes = slice(t * HEADS, (t + 1) * HEADS)
        part = jnp.dot(nm_ref[...], wm_ref[:, :, :, lanes].reshape(SEQ * LANES, HEADS), preferred_element_type=F32)
        part = part + jnp.dot(nr_ref[...], wr_ref[:, :, :, lanes].reshape(SEQ * REST, HEADS), preferred_element_type=F32)
        part = part.astype(BF16)
        if t == 0:
            q_ref[...] = part
        else:
            for s in range(SIDE):
                kv_ref[s, :, (t - 1) * HEADS : t * HEADS] = part


def attend_kernel(row_ref, order_ref, q_ref, kv_ref, stale_ref, out_ref, low_ref, high_ref):
    i = row_ref[0]
    for pair in range(SIDE // 2):
        where, queries, keys, values = [], [], [], []
        for h in (2 * pair, 2 * pair + 1):
            new, old = [], []
            for part in range(2):
                lanes = tile(part * SIDE + h)
                halves = [slice(g * ROWS, (g + 1) * ROWS) for g in range(GROUP)]
                new.append([kv_ref[n % SIDE, halves[n // SIDE], lanes] for n in range(PATCHES)])
                old.append([stale_ref[h, patch_at(order_ref, n, MODS + part * ALL), :] for n in range(PATCHES)])
            for g in range(GROUP):
                where.append((halves[g], tile(h)))
                queries.append(q_ref[halves[g], tile(h)])
                for part, found in ((0, keys), (1, values)):
                    rows = [jnp.where(n <= i + SIDE * g, new[part][n], old[part][n]) for n in range(PATCHES)]
                    found.append(jnp.concatenate(rows, axis=0))
        for (rows, lanes), mixed in zip(where, softmax_mix(queries, keys, values), strict=True):
            for s in range(SIDE):
                out_ref[s, rows, lanes] = mixed
    for part in range(2):
        lanes = pl.ds(pl.multiple_of(part * HEADS + i * HEAD_DIM, HEAD_DIM), HEAD_DIM)
        for n in range(SIDE):
            low_ref[part, n * ROWS : (n + 1) * ROWS, :] = kv_ref[n, :ROWS, lanes]
            high_ref[part, n * ROWS : (n + 1) * ROWS, :] = kv_ref[n, ROWS:, lanes]


def update_kernel(row_ref, mixed_ref, w_ref, below_ref, above_ref, *refs):
    across_low_ref, across_high_ref, x_ref, mods_ref, out_ref, part_ref, held_ref, sems = refs
    i = row_ref[0]
    width = SEQ * HEAD_DIM
    sources = (
        (w_ref, 0, width, i),
        (below_ref, 0, width, lax.rem(i + 3, SIDE)),
        (above_ref, 0, width, lax.rem(i + 1, SIDE)),
        (across_low_ref, 0, width // 2, lax.rem(i + 2, SIDE)),
        (across_high_ref, width // 2, width, lax.rem(i + 2, SIDE)),
    )
    copies = []
    for source, begin, end, h in sources:
        first = pl.ds(pl.multiple_of(h * LANES, LANES), LANES)
        last = pl.ds(pl.multiple_of(SIDE * LANES + h * REST, REST), REST)
        for taken, rows in ((slice(0, LANES), first), (slice(LANES, SHARD), last)):
            held = held_ref.at[rows, begin:end]
            copies.append(pltpu.make_async_copy(source.at[taken, :], held, sems.at[len(copies)]))
    for copy in copies:
        copy.start()
    mixed = jnp.concatenate([mixed_ref[h % SIDE, :, tile(h // SIDE)] for h in range(SEQ)], axis=1)
    for copy in copies:
        copy.wait()
    made = lax.dot_general(mixed, held_ref[...], TRANSPOSED, preferred_element_type=F32)
    mods = mods_ref[...].astype(F32)
    new = x_ref[...].astype(F32) + (mods[4:5] + mods[5:6]) * made
    out_ref[...] = new.astype(BF16)
    for n in range(SIDE):
        rest = new[:, tile(SIDE + n // 2)]
        part_ref[n, :, :LANES] = new[:, tile(n)].astype(BF16)
        part_ref[n, :, LANES:] = (rest if n % 2 == 0 else pltpu.roll(rest, REST, 1)).astype(BF16)


def finish_kernel(order_ref, low_ref, high_ref, kv_low_ref, kv_high_ref, out_ref, cache_ref, rows_ref):
    for half, (x_ref, kv_ref) in enumerate(((low_ref, kv_low_ref), (high_ref, kv_high_ref))):
        for n in range(SIDE):
            at = patch_at(order_ref, half * SIDE + n)
            rows_ref[at, :] = x_ref[n].astype(F32)
            for part in range(2):
                cache_ref[part, at, :] = kv_ref[part, n * ROWS : (n + 1) * ROWS, :]
    out_ref[...] = rows_ref[...].T[:SHARD, :].astype(BF16)


def blank(*shapes):
    return pl.pallas_call(lambda *refs: None, out_shape=shapes, out_specs=(ANY,) * len(shapes), name="blank")()


def body(latents, patch_order, timestep, mod_table, w_qkv, w_out, kv_cache):
    sections = lax.axis_size("section")
    section = lax.axis_index("section")
    position = section % CHAIN
    core = (section % 2).astype(jnp.int32)
    row = (lax.axis_index("seq") // SIDE).astype(jnp.int32)[None]
    w_own = jnp.transpose(w_qkv[0], (1, 0, 2))
    o_own = jnp.transpose(w_out[0], (1, 0))
    cache_own = kv_cache[0]
    mod_now = lax.dynamic_index_in_dim(mod_table, timestep[0], 0, keepdims=False)[0]

    def swap(value):
        return lax.ppermute(value, "section", [(s, s ^ 1) for s in range(sections)])

    def exchange(value, groups):
        return lax.all_to_all(value, "seq", 0, 0, axis_index_groups=groups)

    def shift(value, by):
        pairs = [(s, (s + SIDE * by) % SEQ) for s in range(SEQ)]
        return lax.ppermute(value, "seq", pairs)

    def by_core(value, even, odd):
        groups = [[s * SEQ + d for d in g] for s in range(sections) for g in (odd if s % 2 else even)]
        return lax.all_to_all(value, ("section", "seq"), 0, 0, axis_index_groups=groups)

    def gather_mixed(spread):
        near = by_core(spread, ALONG_Z, ALONG_X)
        far = by_core(jnp.broadcast_to(near[None], (SIDE,) + near.shape), ALONG_X, ALONG_Z)
        return far.reshape((SEQ,) + near.shape[1:])

    def gather(value, groups):
        return exchange(jnp.broadcast_to(value[None], (SIDE,) + value.shape), groups)

    rows_shape, kv_shape = shaped(SIDE, ROWS, 2 * LANES), shaped(2, HALF, HEAD_DIM)
    patch_shape, x_shape, parts_shape = shaped(ROWS, WIDE), shaped(PART, WIDE), shaped(SIDE, PART, 2 * LANES)

    flags = jnp.stack([core == 0, core == 1, core]).astype(jnp.int32)
    flags, mod_now = lax.optimization_barrier((flags, mod_now))
    own, send = call(
        pack_kernel,
        "pack",
        (shaped(PACK, LANES), shaped(CACHE + 2 * ALL, LANES)),
        [SMEM, VMEM, VMEM, VMEM],
        patch_order,
        jnp.transpose(latents[0], (1, 0)),
        mod_now,
        cache_own,
        scratch=[pltpu.VMEM((ALL, 2 * LANES), F32)],
    )
    own, send, w_own, o_own = lax.optimization_barrier((own, send, w_own, o_own))
    got, w_peer, o_peer = swap(send), swap(w_own), swap(o_own)
    got, w_peer, o_peer = lax.optimization_barrier((got, w_peer, o_peer))

    def first_blocks(own, send, got, w_peer, o_peer):
        spread_shape = shaped(SIDE, PACK + MODS, LANES)
        x, spread = call(
            start_kernel, "start", (shaped(PACK, LANES), spread_shape), [SMEM, VMEM, VMEM, VMEM], flags, own, send, got
        )
        kept = []
        for t in range(2):
            q, kv = call(
                functools.partial(project_half_kernel, t),
                "project_half",
                (shaped(HALF, HEAD_DIM), kv_shape),
                [SMEM, VMEM, ANY, ANY],
                flags,
                gather_mixed(spread),
                w_own.reshape(3, SEQ, SHARD, HEAD_DIM),
                w_peer.reshape(3, SEQ, SHARD, HEAD_DIM),
                scratch=[
                    pltpu.VMEM((SEQ, LANES, 3 * HEAD_DIM), BF16),
                    pltpu.VMEM((SEQ, REST, 3 * HEAD_DIM), BF16),
                    pltpu.VMEM((HALF, SEQ * LANES), BF16),
                    pltpu.VMEM((HALF, SEQ * REST), BF16),
                    pltpu.SemaphoreType.DMA((6,)),
                ],
            )
            kv_other = swap(kv)
            mixed = call(
                functools.partial(attend_half_kernel, t),
                "attend_half",
                shaped(SIDE, HALF, HEAD_DIM),
                [SMEM, SMEM, VMEM, VMEM, VMEM, VMEM, VMEM],
                flags,
                patch_order,
                q,
                kv,
                kv_other,
                cache_own,
                got,
            )
            heads = gather_mixed(mixed)
            last = t == 1
            results = call(
                functools.partial(update_half_kernel, t),
                "update_half",
                (rows_shape,) + (() if last else (shaped(PACK, LANES), spread_shape)),
                [SMEM, VMEM, ANY, ANY, VMEM, VMEM, VMEM],
                flags,
                heads,
                o_own,
                o_peer,
                x,
                send,
                got,
                scratch=[
                    pltpu.VMEM(o_own.shape, BF16),
                    pltpu.VMEM((HALF, 2 * LANES), F32),
                    pltpu.SemaphoreType.DMA,
                ],
            )
            if not last:
                x, spread = results[1:]
            kept.append((results[0], kv, kv_other))
        patch = call(join_kernel, "join", patch_shape, [VMEM], exchange(kept[1][0], ALONG_X))
        return patch, kept

    half_width = SEQ * HEAD_DIM // 2

    def prepare(small):
        w = w_own.reshape(3, SIDE, SIDE, SHARD, HEAD_DIM)
        w_near = shift(w, 1), shift(w, -1)
        small = gather(small, ALONG_X)
        mods = call(mods_kernel, "mods", shaped(MODS, WIDE), [VMEM], small)
        others = gather(mods, ALONG_Z), small, mods
        w_near, o, others = lax.optimization_barrier((w_near, o_own, others))
        w_far = shift(w_near[0][:, : SIDE // 2], 1), shift(w_near[1][:, SIDE // 2 :], -1)
        o_near = shift(o, 1), shift(o, -1)
        w_far, o_near = lax.optimization_barrier((w_far, o_near))
        o_far = shift(o_near[0][:, :half_width], 1), shift(o_near[1][:, half_width:], -1)
        mods_all, small, mods = others
        return w_near + w_far, o_near + o_far, small, mods, mods_all

    def no_weights(small):
        side, half = (shaped(3, n, SIDE, SHARD, HEAD_DIM) for n in (SIDE, SIDE // 2))
        whole, part = (shaped(SHARD, n) for n in (2 * half_width, half_width))
        shapes = (side, side, half, half, whole, whole, part, part)
        shapes += (shaped(SIDE, *small.shape), shaped(MODS, WIDE), shaped(SIDE, MODS, WIDE))
        made = blank(*shapes)
        return tuple(made[:4]), tuple(made[4:8]), *made[8:]

    def later_block(x, spread, w_others, o_others, small, mods, mods_all):
        q, kv = call(
            project_kernel,
            "project",
            (shaped(PART, HEADS), shaped(SIDE, PART, 2 * HEADS)),
            [SMEM, VMEM, VMEM] + [ANY] * 5,
            row,
            exchange(spread, ALONG_Z),
            mods_all,
            w_own.reshape(3, SIDE, SIDE, SHARD, HEAD_DIM),
            *w_others,
            scratch=[
                pltpu.VMEM((SIDE, SIDE, LANES, 3 * HEADS), BF16),
                pltpu.VMEM((SIDE, SIDE, REST, 3 * HEADS), BF16),
                pltpu.VMEM((PART, SEQ * LANES), BF16),
                pltpu.VMEM((PART, SEQ * REST), BF16),
                pltpu.SemaphoreType.DMA((75,)),
            ],
            mib=20,
        )
        mixed, kv_low, kv_high = call(
            attend_kernel,
            "attend",
            (shaped(SIDE, PART, HEADS), kv_shape, kv_shape),
            [SMEM, SMEM, VMEM, VMEM, VMEM],
            row,
            patch_order,
            q,
            exchange(kv, ALONG_X),
            small,
        )
        new, parts = call(
            update_kernel,
            "update",
            (x_shape, parts_shape),
            [SMEM, VMEM] + [ANY] * 5 + [VMEM, VMEM],
            row,
            exchange(mixed, ALONG_Z),
            o_own,
            *o_others,
            x,
            mods,
            scratch=[pltpu.VMEM((WIDE, SEQ * HEAD_DIM), BF16), pltpu.SemaphoreType.DMA((10,))],
        )
        return new, parts, kv_low, kv_high

    def second_block(low, high, weights):
        spread_shape = shaped(SIDE, PART, WIDE)
        x, spread = call(spread_kernel, "spread", (x_shape, spread_shape), [VMEM, VMEM], low, high)
        return later_block(x, spread, *weights)

    def third_block(x, weights):
        return later_block(x, jnp.broadcast_to(x[None], (SIDE,) + x.shape), *weights)

    early = position < 2
    one = (rows_shape, kv_shape, kv_shape)

    def not_here(*_):
        patch, *both = blank(patch_shape, *one, *one)
        return patch, [tuple(both[:3]), tuple(both[3:])]

    patch, kept = lax.cond(early, first_blocks, not_here, own, send, got, w_peer, o_peer)
    weights = lax.cond(early, no_weights, prepare, send[PACK:])
    patch, weights = lax.optimization_barrier((patch, weights))
    low = lax.ppermute(patch, "section", [(s, s + 2) for s in range(sections) if s % CHAIN == 0])
    high = lax.ppermute(patch, "section", [(s, s + 1) for s in range(sections) if s % CHAIN == 1])
    state = blank(x_shape, parts_shape, kv_shape, kv_shape)
    state = lax.cond(
        position == 2,
        lambda low, high, state, weights: second_block(low, high, weights),
        lambda low, high, state, weights: tuple(state),
        low,
        high,
        tuple(state),
        weights,
    )
    arrived = lax.ppermute(state[0], "section", [(s, s + 1) for s in range(sections) if s % CHAIN == 2])
    state = lax.cond(
        position == 3,
        lambda x, state, weights: third_block(x, weights)[1:],
        lambda x, state, weights: tuple(state),
        arrived,
        tuple(state[1:]),
        weights,
    )

    def finish_early(state, kept):
        (rows0, kv0, other0), (rows1, kv1, other1) = kept
        first = core == 0
        mine, theirs = jnp.where(first, rows0, rows1), jnp.where(first, rows1, rows0)
        other = swap(theirs)
        rows = jnp.where(first, mine, other), jnp.where(first, other, mine)
        return rows + (jnp.where(first, kv0, other1), jnp.where(first, other0, kv1))

    def finish_late(state, kept):
        parts, kv_low, kv_high = state
        rows = exchange(parts, ALONG_X)
        return rows[:, :ROWS], rows[:, ROWS:], kv_low, kv_high

    rows_low, rows_high, kv_low, kv_high = lax.cond(early, finish_early, finish_late, state, kept)
    out_t, cache = call(
        finish_kernel,
        "finish",
        (shaped(SHARD, ALL), shaped(2, ALL, HEAD_DIM)),
        [SMEM, VMEM, VMEM, VMEM, VMEM],
        patch_order,
        rows_low,
        rows_high,
        kv_low,
        kv_high,
        scratch=[pltpu.VMEM((ALL, 2 * LANES), F32)],
    )
    return jnp.transpose(out_t, (1, 0))[None], cache[None]


def solution(mesh):
    return jax.shard_map(
        body,
        mesh=mesh,
        in_specs=(
            P("section", None, "seq"),
            P(),
            P(),
            P(None, "section", None, "seq"),
            P("section", None, None, "seq"),
            P("section", None, "seq"),
            P("section", None, None, "seq"),
        ),
        out_specs=(P("section", None, "seq"), P("section", None, None, "seq")),
        check_vma=False,
    )
```

```python
import functools

import jax
import jax.numpy as jnp
from jax import lax
from jax.experimental import pallas as pl
from jax.experimental.pallas import tpu as pltpu
from jax.sharding import PartitionSpec as P

HEAD_DIM = 128
PATCHES = 8
CHAIN = 4
EPSILON = 1e-06
ROWS = 64
ALL = PATCHES * ROWS
SIDE = 4
SEQ = SIDE * SIDE
LANES = 128
REST = 64
SHARD = LANES + REST
WIDTH = SEQ * SHARD
HALF = ALL // 2
QUARTER = HALF // 2
PACK = HALF + QUARTER
PIECE = ROWS + ROWS // 2
MODS = 16
CACHE = PACK + MODS
GROUP = PATCHES // SIDE
PART = GROUP * ROWS
WIDE = SIDE * SHARD
HEADS = SIDE * HEAD_DIM
SCALE = HEAD_DIM ** (-0.5)
F32 = jnp.float32
BF16 = jnp.bfloat16
VMEM = pl.BlockSpec(memory_space=pltpu.VMEM)
SMEM = pl.BlockSpec(memory_space=pltpu.SMEM)
ANY = pl.BlockSpec(memory_space=pl.ANY)
ALONG_X = [[SIDE * i + j for i in range(SIDE)] for j in range(SIDE)]
ALONG_Z = [[SIDE * i + j for j in range(SIDE)] for i in range(SIDE)]
TRANSPOSED = (((1,), (1,)), ((), ()))


def shaped(*shape, dtype=BF16):
    return jax.ShapeDtypeStruct(shape, dtype)


def call(kernel, name, out_shape, in_specs, *args, scratch=(), mib=12, outside=()):
    many = isinstance(out_shape, tuple)
    spaces = [ANY if n in outside else VMEM for n in range(len(out_shape) if many else 1)]
    return pl.pallas_call(
        kernel,
        out_shape=out_shape,
        in_specs=in_specs,
        out_specs=tuple(spaces) if many else spaces[0],
        scratch_shapes=list(scratch),
        compiler_params=pltpu.CompilerParams(vmem_limit_bytes=mib * 1024 * 1024),
        name=name,
    )(*args)


def low_lanes(rows):
    return lax.broadcasted_iota(jnp.int32, (rows, LANES), 1) < REST


def patch_at(order_ref, j, base=0):
    return pl.ds(pl.multiple_of(base + order_ref[j] * ROWS, ROWS), ROWS)


def tile(k):
    return slice(k * LANES, (k + 1) * LANES)


def pair_lanes(low, even, odd):
    return jnp.where(low, even, pltpu.roll(odd, REST, 1))


def softmax_mix(queries, keys, values):
    scores = [
        lax.dot_general(q, k, TRANSPOSED, preferred_element_type=F32) * SCALE for q, k in zip(queries, keys, strict=True)
    ]
    tops = [jnp.max(x, axis=1, keepdims=True) for x in scores]
    terms = [jnp.exp(x - top) for x, top in zip(scores, tops, strict=True)]
    sums = [jnp.sum(x, axis=1, keepdims=True) for x in terms]
    weights = [(x * (1.0 / total)).astype(BF16) for x, total in zip(terms, sums, strict=True)]
    return [jnp.dot(w, v, preferred_element_type=F32).astype(BF16) for w, v in zip(weights, values, strict=True)]


def pack_kernel(order_ref, lat_ref, mod_ref, cache_ref, own_ref, send_ref, rows_ref):
    rows_ref[:, :SHARD] = lat_ref[...].astype(F32).T
    low = low_lanes(ROWS)
    for core, out_ref in ((0, own_ref), (1, send_ref)):
        rest = []
        for j in range(SIDE):
            at = patch_at(order_ref, core * SIDE + j)
            out_ref[j * ROWS : (j + 1) * ROWS, :] = rows_ref[at, :LANES].astype(BF16)
            rest.append(rows_ref[at, LANES:])
        for j in range(2):
            both = pair_lanes(low, rest[j], rest[j + 2])
            out_ref[HALF + j * ROWS : HALF + (j + 1) * ROWS, :] = both.astype(BF16)
    mod = mod_ref[...]
    lines = []
    for kind in (1.0 + mod[1:2], mod[0:1], mod[2:3]):
        last = jnp.concatenate([kind[:, LANES:], kind[:, LANES:]], axis=1)
        for value in (kind[:, :LANES], last):
            high = value.astype(BF16).astype(F32)
            lines += [high, value - high]
    lines.append(jnp.zeros((MODS - len(lines), LANES), F32))
    send_ref[PACK : PACK + MODS, :] = jnp.concatenate(lines, axis=0).astype(BF16)
    for part in range(2):
        send_ref[CACHE + part * ALL : CACHE + (part + 1) * ALL, :] = cache_ref[part]


def mods_of(flag_ref, t, send_ref, got_ref):
    return jnp.where(flag_ref[t] == 1, send_ref[PACK:CACHE, :], got_ref[PACK:CACHE, :])


def start_kernel(flag_ref, own_ref, send_ref, got_ref, x_ref, out_ref):
    x = jnp.where(flag_ref[2] == 0, own_ref[...], got_ref[:PACK, :])
    mods = mods_of(flag_ref, 0, send_ref, got_ref)
    x_ref[...] = x
    for s in range(SIDE):
        out_ref[s, :PACK, :] = x
        out_ref[s, PACK:, :] = mods


def place(flag_ref, s):
    return jnp.where(flag_ref[2] == 0, s, (s % SIDE) * SIDE + s // SIDE)


def project_half_kernel(t_now, flag_ref, x_ref, own_ref, peer_ref, q_ref, kv_ref, wm_ref, wr_ref, nm_ref, nr_ref, sems):
    def copies(w_ref):
        found = []
        for t in range(3):
            lanes = pl.ds(t * HEAD_DIM, HEAD_DIM)
            found.append(pltpu.make_async_copy(w_ref.at[t, :, :LANES, :], wm_ref.at[:, :, lanes], sems.at[2 * t]))
            found.append(pltpu.make_async_copy(w_ref.at[t, :, LANES:, :], wr_ref.at[:, :, lanes], sems.at[2 * t + 1]))
        return found

    @pl.when(flag_ref[t_now] == 1)
    def _():
        for copy in copies(own_ref):
            copy.start()

    @pl.when(flag_ref[t_now] == 0)
    def _():
        for copy in copies(peer_ref):
            copy.start()

    low = low_lanes(ROWS)
    at = [place(flag_ref, s) for s in range(SEQ)]

    def line(s, k):
        pair = x_ref[at[s], PACK:, :].astype(F32)
        return pair[2 * k : 2 * k + 1] + pair[2 * k + 1 : 2 * k + 2]

    scale_first = [line(s, 0) for s in range(SEQ)]
    shift_first = [line(s, 2) for s in range(SEQ)]
    scale_last = [jnp.where(low[:1], line(2 * p, 1), line(2 * p + 1, 1)) for p in range(SEQ // 2)]
    shift_last = [jnp.where(low[:1], line(2 * p, 3), line(2 * p + 1, 3)) for p in range(SEQ // 2)]
    for j in range(SIDE):
        mine = pl.ds(j * ROWS, ROWS)
        rest = pl.ds(HALF + (j % 2) * ROWS, ROWS)
        total = jnp.zeros((ROWS, LANES), F32)
        square = jnp.zeros((ROWS, LANES), F32)
        total_rest = jnp.zeros((ROWS, LANES), F32)
        square_rest = jnp.zeros((ROWS, LANES), F32)
        for s in range(SEQ):
            x = x_ref[at[s], mine, :].astype(F32)
            total = total + x
            square = square + x * x
            x = x_ref[at[s], rest, :].astype(F32)
            total_rest = total_rest + x
            square_rest = square_rest + x * x
        in_half = low if j < 2 else jnp.logical_not(low)
        total = total + jnp.where(in_half, total_rest, 0.0)
        square = square + jnp.where(in_half, square_rest, 0.0)
        mean = jnp.sum(total, axis=1, keepdims=True) / WIDTH
        var = jnp.sum(square, axis=1, keepdims=True) / WIDTH - mean * mean
        rstd = lax.rsqrt(var + EPSILON)
        for s in range(SEQ):
            x = x_ref[at[s], mine, :].astype(F32)
            normed = (x - mean) * rstd * scale_first[s] + shift_first[s]
            nm_ref[mine, tile(s)] = normed.astype(BF16)
        for p in range(SEQ // 2):
            even = x_ref[at[2 * p], rest, :].astype(F32)
            odd = x_ref[at[2 * p + 1], rest, :].astype(F32)
            if j < 2:
                x = pair_lanes(low, even, odd)
            else:
                x = jnp.where(low, pltpu.roll(even, REST, 1), odd)
            normed = (x - mean) * rstd * scale_last[p] + shift_last[p]
            nr_ref[mine, tile(p)] = normed.astype(BF16)

    for copy in copies(own_ref):
        copy.wait()
    w_first = wm_ref[...].reshape(SEQ * LANES, 3 * HEAD_DIM)
    w_last = wr_ref[...].reshape(SEQ * REST, 3 * HEAD_DIM)
    qkv = jnp.dot(nm_ref[...], w_first, preferred_element_type=F32)
    qkv = qkv + jnp.dot(nr_ref[...], w_last, preferred_element_type=F32)
    qkv = qkv.astype(BF16)
    q_ref[...] = qkv[:, :HEAD_DIM]
    kv_ref[0] = qkv[:, HEAD_DIM : 2 * HEAD_DIM]
    kv_ref[1] = qkv[:, 2 * HEAD_DIM :]


def attend_half_kernel(t, flag_ref, order_ref, q_ref, kv_ref, other_ref, own_ref, got_ref, *refs):
    o_own_ref, o_peer_ref, out_ref, w_ref, sem = refs

    @pl.when(flag_ref[t] == 1)
    def _():
        pltpu.make_async_copy(o_own_ref, w_ref, sem).start()

    @pl.when(flag_ref[t] == 0)
    def _():
        pltpu.make_async_copy(o_peer_ref, w_ref, sem).start()

    mine = flag_ref[t] == 1
    core = flag_ref[2]

    def stale(part, j):
        peer = got_ref[patch_at(order_ref, j, CACHE + part * ALL), :]
        return jnp.where(mine, own_ref[part, patch_at(order_ref, j), :], peer)

    old, other = [], []
    for part in range(2):
        old.append([stale(part, core * SIDE + j) for j in range(SIDE)])
        kept = jnp.concatenate([stale(part, (1 - core) * SIDE + j) for j in range(SIDE)], axis=0)
        other.append(jnp.where(core == 1, other_ref[part], kept))
    queries, keys, values = [], [], []
    for j in range(SIDE):
        queries.append(q_ref[j * ROWS : (j + 1) * ROWS, :])
        for part, found in ((0, keys), (1, values)):
            parts = [kv_ref[part, : (j + 1) * ROWS, :]] + old[part][j + 1 :] + [other[part]]
            found.append(jnp.concatenate(parts, axis=0))
    for j, mixed in enumerate(softmax_mix(queries, keys, values)):
        for s in range(SIDE):
            out_ref[s, j * ROWS : (j + 1) * ROWS, :] = mixed
    pltpu.make_async_copy(o_own_ref, w_ref, sem).wait()


def update_half_kernel(t, flag_ref, mixed_ref, w_ref, x_ref, send_ref, got_ref, rows_out_ref, *refs):
    last = t == 1
    if last:
        hand_out_ref, held_ref, rows_ref, hand_ref, sems = refs
    else:
        new_ref, spread_ref, held_ref, rows_ref, _, sems = refs

    mixed = jnp.concatenate([mixed_ref[place(flag_ref, h)] for h in range(SEQ)], axis=1)
    held_ref[:, :SHARD] = lax.dot_general(mixed, w_ref[...], TRANSPOSED, preferred_element_type=F32)
    mods = mods_of(flag_ref, t, send_ref, got_ref).astype(F32)
    gate_first = mods[8:9] + mods[9:10]
    gate_last = mods[10:11] + mods[11:12]
    first = (x_ref[:HALF, :].astype(F32) + gate_first * held_ref[:, :LANES]).astype(BF16)
    made = pair_lanes(low_lanes(QUARTER), held_ref[:QUARTER, LANES:], held_ref[QUARTER:, LANES:])
    rest = x_ref[HALF:, :].astype(F32) + gate_last * made
    other = pltpu.roll(rest, REST, 1)
    if last:
        for n in range(SIDE):
            lines = (rest if n < 2 else other)[(n % 2) * ROWS : (n % 2 + 1) * ROWS]
            hand_ref[n, :ROWS, :] = first[n * ROWS : (n + 1) * ROWS]
            both = pair_lanes(low_lanes(ROWS // 2), lines[: ROWS // 2], lines[ROWS // 2 :])
            hand_ref[n, ROWS:, :] = both.astype(BF16)
        out = [pltpu.make_async_copy(hand_ref, hand_out_ref, sems.at[1])]
        out[0].start()
    else:
        out = []
    other = other.astype(BF16)
    rest = rest.astype(BF16)
    for n in range(SIDE):
        at = slice((n % 2) * ROWS, (n % 2 + 1) * ROWS)
        rows_ref[n, :, :LANES] = first[n * ROWS : (n + 1) * ROWS]
        rows_ref[n, :, LANES:] = rest[at] if n < 2 else other[at]
    out.append(pltpu.make_async_copy(rows_ref, rows_out_ref, sems.at[0]))
    out[-1].start()
    if not last:
        mods = mods_of(flag_ref, 1, send_ref, got_ref)
        new_ref[:HALF, :] = first
        new_ref[HALF:, :] = rest
        for s in range(SIDE):
            spread_ref[s, :HALF, :] = first
            spread_ref[s, HALF:PACK, :] = rest
            spread_ref[s, PACK:, :] = mods
    for copy in out:
        copy.wait()


def mods_kernel(gathered_ref, out_ref):
    low = low_lanes(1)
    rows = [gathered_ref[i, :MODS, :].astype(F32) for i in range(SIDE)]
    lines = []
    for k in range(3):
        for h in range(2):
            first, last = 4 * k + h, 4 * k + 2 + h
            parts = [rows[i][first : first + 1] for i in range(SIDE)]
            for m in range(SIDE // 2):
                even, odd = (rows[2 * m + e][last : last + 1] for e in range(2))
                parts.append(jnp.where(low, even, odd))
            lines.append(jnp.concatenate(parts, axis=1))
    lines.append(jnp.zeros((MODS - len(lines), WIDE), F32))
    out_ref[...] = jnp.concatenate(lines, axis=0).astype(BF16)


def spread_kernel(low_ref, high_ref, out_ref):
    for s in range(SEQ):
        out_ref[s, :PIECE, :] = low_ref[s // SIDE]
        out_ref[s, PIECE:, :] = high_ref[s // SIDE]


def unpack(even, odd):
    low = low_lanes(ROWS // 2)
    return jnp.concatenate([pair_lanes(low, even, odd), jnp.where(low, pltpu.roll(even, REST, 1), odd)], axis=0)


def project_kernel(packed, row_ref, x_ref, mods_ref, w_ref, below_ref, above_ref, *refs):
    across_low_ref, across_high_ref, q_ref, kv_ref, *refs = refs
    if packed:
        keep_out_ref, *refs = refs
    wm_ref, wr_ref, nm_ref, nr_ref, keep_ref, sems = refs
    i = row_ref[0]
    half = SIDE // 2
    sources = (
        (w_ref, 0, SIDE, i),
        (below_ref, 0, SIDE, lax.rem(i + 3, SIDE)),
        (above_ref, 0, SIDE, lax.rem(i + 1, SIDE)),
        (across_low_ref, 0, half, lax.rem(i + 2, SIDE)),
        (across_high_ref, half, SIDE, lax.rem(i + 2, SIDE)),
    )
    copies = []
    for t in range(3):
        for source, first, last, h in sources:
            lanes = pl.ds(pl.multiple_of((t * SIDE + h) * HEAD_DIM, HEAD_DIM), HEAD_DIM)
            pairs = [(source.at[t, :, :, :LANES, :], wm_ref.at[first:last, :, :, lanes])]
            pairs += [(source.at[t, :, j, LANES:, :], wr_ref.at[j, first:last, :, lanes]) for j in range(SIDE)]
            copies += [pltpu.make_async_copy(a, b, sems.at[len(copies) + n]) for n, (a, b) in enumerate(pairs)]
    for copy in copies:
        copy.start()
    mods = [mods_ref[j].astype(F32) for j in range(SIDE)]
    scale = [m[0:1] + m[1:2] for m in mods]
    shift = [m[2:3] + m[3:4] for m in mods]
    tiles = WIDE // LANES

    def features(g, j, k):
        if not packed:
            return x_ref[j, g * ROWS : (g + 1) * ROWS, tile(k)].astype(F32)
        if k < SIDE:
            return x_ref[k * SIDE + j, g * PIECE : g * PIECE + ROWS, :].astype(F32)
        pair = (2 * (k - SIDE) * SIDE + j, (2 * (k - SIDE) + 1) * SIDE + j)
        return unpack(*(x_ref[s, g * PIECE + ROWS : (g + 1) * PIECE, :].astype(F32) for s in pair))

    for g in range(GROUP):
        mine = pl.ds(g * ROWS, ROWS)
        total, square = (jnp.zeros((ROWS, LANES), F32) for _ in range(2))
        for j in range(SIDE):
            for k in range(tiles):
                x = features(g, j, k)
                total = total + x
                square = square + x * x
        mean = jnp.sum(total, axis=1, keepdims=True) / WIDTH
        var = jnp.sum(square, axis=1, keepdims=True) / WIDTH - mean * mean
        rstd = lax.rsqrt(var + EPSILON)
        for j in range(SIDE):
            for k in range(tiles):
                x = features(g, j, k)
                normed = ((x - mean) * rstd * scale[j][:, tile(k)] + shift[j][:, tile(k)]).astype(BF16)
                if k < SIDE:
                    nm_ref[mine, tile(k * SIDE + j)] = normed
                else:
                    nr_ref[mine, tile(j * (SIDE // 2) + k - SIDE)] = normed
        if packed:
            for k in range(tiles):
                keep_ref[mine, tile(k)] = features(g, row_ref[1], k).astype(BF16)
    kept = [pltpu.make_async_copy(keep_ref, keep_out_ref, sems.at[len(copies)])] if packed else []
    for copy in kept:
        copy.start()
    each = len(copies) // 3
    for t in range(3):
        for copy in copies[t * each : (t + 1) * each]:
            copy.wait()
        lanes = slice(t * HEADS, (t + 1) * HEADS)
        part = jnp.dot(nm_ref[...], wm_ref[:, :, :, lanes].reshape(SEQ * LANES, HEADS), preferred_element_type=F32)
        part = part + jnp.dot(nr_ref[...], wr_ref[:, :, :, lanes].reshape(SEQ * REST, HEADS), preferred_element_type=F32)
        part = part.astype(BF16)
        if t == 0:
            q_ref[...] = part
        else:
            for s in range(SIDE):
                kv_ref[s, :, (t - 1) * HEADS : t * HEADS] = part
    for copy in kept:
        copy.wait()


def load_out(i, w_ref, below_ref, above_ref, across_low_ref, across_high_ref, held_ref, sems):
    width = SEQ * HEAD_DIM
    sources = (
        (w_ref, 0, width, i),
        (below_ref, 0, width, lax.rem(i + 3, SIDE)),
        (above_ref, 0, width, lax.rem(i + 1, SIDE)),
        (across_low_ref, 0, width // 2, lax.rem(i + 2, SIDE)),
        (across_high_ref, width // 2, width, lax.rem(i + 2, SIDE)),
    )
    copies = []
    for source, begin, end, h in sources:
        first = pl.ds(pl.multiple_of(h * LANES, LANES), LANES)
        last = pl.ds(pl.multiple_of(SIDE * LANES + h * REST, REST), REST)
        for taken, rows in ((slice(0, LANES), first), (slice(LANES, SHARD), last)):
            held = held_ref.at[rows, begin:end]
            copies.append(pltpu.make_async_copy(source.at[taken, :], held, sems.at[len(copies)]))
    return copies


def attend_kernel(row_ref, order_ref, q_ref, kv_ref, stale_ref, *refs):
    *w_refs, out_ref, held_ref, low_ref, high_ref, sems = refs
    i = row_ref[0]
    copies = load_out(i, *w_refs, held_ref, sems)
    for part in range(2):
        lanes = pl.ds(pl.multiple_of(part * HEADS + i * HEAD_DIM, HEAD_DIM), HEAD_DIM)
        for n in range(SIDE):
            for half, own_ref in enumerate((low_ref, high_ref)):
                new = kv_ref.at[n, half * ROWS : (half + 1) * ROWS, lanes]
                own = own_ref.at[part, n * ROWS : (n + 1) * ROWS, :]
                copies.append(pltpu.make_async_copy(new, own, sems.at[len(copies)]))
    for copy in copies:
        copy.start()
    for pair in range(SIDE // 2):
        where, queries, keys, values = [], [], [], []
        for h in (2 * pair, 2 * pair + 1):
            new, old = [], []
            for part in range(2):
                lanes = tile(part * SIDE + h)
                halves = [slice(g * ROWS, (g + 1) * ROWS) for g in range(GROUP)]
                new.append([kv_ref[n % SIDE, halves[n // SIDE], lanes] for n in range(PATCHES)])
                old.append([stale_ref[h, patch_at(order_ref, n, MODS + part * ALL), :] for n in range(PATCHES)])
            for g in range(GROUP):
                where.append((halves[g], tile(h)))
                queries.append(q_ref[halves[g], tile(h)])
                for part, found in ((0, keys), (1, values)):
                    rows = [jnp.where(n <= i + SIDE * g, new[part][n], old[part][n]) for n in range(PATCHES)]
                    found.append(jnp.concatenate(rows, axis=0))
        for (rows, lanes), mixed in zip(where, softmax_mix(queries, keys, values), strict=True):
            for s in range(SIDE):
                out_ref[s, rows, lanes] = mixed
    for copy in copies:
        copy.wait()


def update_kernel(last, mixed_ref, held_ref, x_in_ref, mods_in_ref, *refs):
    if not last:
        out_ref, *refs = refs
    part_ref, x_ref, mods_ref, made_ref, cut_ref, sems = refs
    copies = []
    copies.append(pltpu.make_async_copy(x_in_ref, x_ref, sems.at[len(copies)]))
    copies.append(pltpu.make_async_copy(mods_in_ref, mods_ref, sems.at[len(copies)]))
    for copy in copies:
        copy.start()
    mixed = jnp.concatenate([mixed_ref[h % SIDE, :, tile(h // SIDE)] for h in range(SEQ)], axis=1)
    for copy in copies:
        copy.wait()
    made = lax.dot_general(mixed, held_ref[...], TRANSPOSED, preferred_element_type=F32)
    mods = mods_ref[...].astype(F32)
    new = x_ref[...].astype(F32) + (mods[4:5] + mods[5:6]) * made
    out = []
    if not last:
        made_ref[...] = new.astype(BF16)
        out.append(pltpu.make_async_copy(made_ref, out_ref, sems.at[0]))
        out[0].start()
    for n in range(SIDE):
        rest = new[:, tile(SIDE + n // 2)]
        cut_ref[n, :, :LANES] = new[:, tile(n)].astype(BF16)
        cut_ref[n, :, LANES:] = (rest if n % 2 == 0 else pltpu.roll(rest, REST, 1)).astype(BF16)
    out.append(pltpu.make_async_copy(cut_ref, part_ref, sems.at[1]))
    out[-1].start()
    for copy in out:
        copy.wait()


def finish_kernel(order_ref, low_ref, high_ref, kv_low_ref, kv_high_ref, out_ref, cache_ref, rows_ref):
    for half, (x_ref, kv_ref) in enumerate(((low_ref, kv_low_ref), (high_ref, kv_high_ref))):
        for n in range(SIDE):
            at = patch_at(order_ref, half * SIDE + n)
            rows_ref[at, :] = x_ref[n].astype(F32)
            for part in range(2):
                cache_ref[part, at, :] = kv_ref[part, n * ROWS : (n + 1) * ROWS, :]
    out_ref[...] = rows_ref[...].T[:SHARD, :].astype(BF16)


def blank(*shapes):
    return pl.pallas_call(lambda *refs: None, out_shape=shapes, out_specs=(ANY,) * len(shapes), name="blank")()


def body(latents, patch_order, timestep, mod_table, w_qkv, w_out, kv_cache):
    sections = lax.axis_size("section")
    section = lax.axis_index("section")
    position = section % CHAIN
    core = (section % 2).astype(jnp.int32)
    seq = lax.axis_index("seq").astype(jnp.int32)
    row = jnp.stack([seq // SIDE, seq % SIDE])
    w_own = jnp.transpose(w_qkv[0], (1, 0, 2))
    o_own = jnp.transpose(w_out[0], (1, 0))
    cache_own = kv_cache[0]
    mod_now = lax.dynamic_index_in_dim(mod_table, timestep[0], 0, keepdims=False)[0]

    def swap(value):
        return lax.ppermute(value, "section", [(s, s ^ 1) for s in range(sections) if s % CHAIN < 2])

    def exchange(value, groups):
        return lax.all_to_all(value, "seq", 0, 0, axis_index_groups=groups)

    def shift(value, by):
        pairs = [(s, (s + SIDE * by) % SEQ) for s in range(SEQ)]
        return lax.ppermute(value, "seq", pairs)

    def by_core(value, even, odd):
        groups = [[s * SEQ + d for d in g] for s in range(sections) for g in (odd if s % 2 else even)]
        return lax.all_to_all(value, ("section", "seq"), 0, 0, axis_index_groups=groups)

    def gather_mixed(spread):
        near = by_core(spread, ALONG_Z, ALONG_X)
        far = by_core(jnp.broadcast_to(near[None], (SIDE,) + near.shape), ALONG_X, ALONG_Z)
        return far.reshape((SEQ,) + near.shape[1:])

    def gather(value, groups):
        return exchange(jnp.broadcast_to(value[None], (SIDE,) + value.shape), groups)

    rows_shape, kv_shape = shaped(SIDE, ROWS, 2 * LANES), shaped(2, HALF, HEAD_DIM)
    hand_shape, x_shape, parts_shape = shaped(SIDE, PIECE, LANES), shaped(PART, WIDE), shaped(SIDE, PART, 2 * LANES)

    flags = jnp.stack([core == 0, core == 1, core]).astype(jnp.int32)
    flags, mod_now = lax.optimization_barrier((flags, mod_now))
    own, send = call(
        pack_kernel,
        "pack",
        (shaped(PACK, LANES), shaped(CACHE + 2 * ALL, LANES)),
        [SMEM, VMEM, VMEM, VMEM],
        patch_order,
        jnp.transpose(latents[0], (1, 0)),
        mod_now,
        cache_own,
        scratch=[pltpu.VMEM((ALL, 2 * LANES), F32)],
    )
    own, send, w_own, o_own = lax.optimization_barrier((own, send, w_own, o_own))
    got, w_peer, o_peer = swap(send), swap(w_own), swap(o_own)
    got, w_peer, o_peer = lax.optimization_barrier((got, w_peer, o_peer))

    spread_shape = shaped(SIDE, PACK + MODS, LANES)

    def first_blocks(own, send, got, w_peer, o_peer):
        shapes = shaped(PACK, LANES), spread_shape
        x, spread = call(start_kernel, "start", shapes, [SMEM, VMEM, VMEM, VMEM], flags, own, send, got)
        gathered = gather_mixed(spread)
        kept = []
        for t in range(2):
            q, kv = call(
                functools.partial(project_half_kernel, t),
                "project_half",
                (shaped(HALF, HEAD_DIM), kv_shape),
                [SMEM, VMEM, ANY, ANY],
                flags,
                gathered,
                w_own.reshape(3, SEQ, SHARD, HEAD_DIM),
                w_peer.reshape(3, SEQ, SHARD, HEAD_DIM),
                scratch=[
                    pltpu.VMEM((SEQ, LANES, 3 * HEAD_DIM), BF16),
                    pltpu.VMEM((SEQ, REST, 3 * HEAD_DIM), BF16),
                    pltpu.VMEM((HALF, SEQ * LANES), BF16),
                    pltpu.VMEM((HALF, SEQ * REST), BF16),
                    pltpu.SemaphoreType.DMA((6,)),
                ],
            )
            kv_other = swap(kv)
            mixed, w_now = call(
                functools.partial(attend_half_kernel, t),
                "attend_half",
                (shaped(SIDE, HALF, HEAD_DIM), shaped(*o_own.shape)),
                [SMEM, SMEM, VMEM, VMEM, VMEM, VMEM, VMEM, ANY, ANY],
                flags,
                patch_order,
                q,
                kv,
                kv_other,
                cache_own,
                got,
                o_own,
                o_peer,
                scratch=[pltpu.SemaphoreType.DMA],
            )
            heads = gather_mixed(mixed)
            last = t == 1
            results = call(
                functools.partial(update_half_kernel, t),
                "update_half",
                (rows_shape,) + ((hand_shape,) if last else (shaped(PACK, LANES), spread_shape)),
                [SMEM, VMEM, VMEM, VMEM, VMEM, VMEM],
                flags,
                heads,
                w_now,
                x,
                send,
                got,
                scratch=[
                    pltpu.VMEM((HALF, 2 * LANES), F32),
                    pltpu.VMEM(rows_shape.shape, BF16),
                    pltpu.VMEM(hand_shape.shape, BF16),
                    pltpu.SemaphoreType.DMA((2,)),
                ],
                outside=(0, 1) if last else (0,),
            )
            if not last:
                x, gathered = results[1], gather_mixed(results[2])
            kept.append((results[0], kv, kv_other))
        return results[1], kept

    half_width = SEQ * HEAD_DIM // 2

    def prepare(small):
        w = w_own.reshape(3, SIDE, SIDE, SHARD, HEAD_DIM)
        w_near, o, small = lax.optimization_barrier(((shift(w, 1), shift(w, -1)), o_own, small))
        w_far = shift(w_near[0][:, : SIDE // 2], 1), shift(w_near[1][:, SIDE // 2 :], -1)
        o_near = shift(o, 1), shift(o, -1)
        small = gather(small, ALONG_X)
        mods = call(mods_kernel, "mods", shaped(MODS, WIDE), [VMEM], small, mib=4)
        others = gather(mods, ALONG_Z), small, mods
        w_far, o_near, others = lax.optimization_barrier((w_far, o_near, others))
        o_far = shift(o_near[0][:, :half_width], 1), shift(o_near[1][:, half_width:], -1)
        mods_all, small, mods = others
        return w_near + w_far, o_near + o_far, small, mods, mods_all

    def no_weights(small):
        side, half = (shaped(3, n, SIDE, SHARD, HEAD_DIM) for n in (SIDE, SIDE // 2))
        whole, part = (shaped(SHARD, n) for n in (2 * half_width, half_width))
        shapes = (side, side, half, half, whole, whole, part, part)
        shapes += (shaped(SIDE, *small.shape), shaped(MODS, WIDE), shaped(SIDE, MODS, WIDE))
        made = blank(*shapes)
        return tuple(made[:4]), tuple(made[4:8]), *made[8:]

    def later_block(x, gathered, w_others, o_others, small, mods, mods_all):
        packed = x is None
        q, kv, *keep = call(
            functools.partial(project_kernel, packed),
            "project",
            (shaped(PART, HEADS), shaped(SIDE, PART, 2 * HEADS)) + (x_shape,) * packed,
            [SMEM, VMEM, VMEM] + [ANY] * 5,
            row,
            gathered,
            mods_all,
            w_own.reshape(3, SIDE, SIDE, SHARD, HEAD_DIM),
            *w_others,
            scratch=[
                pltpu.VMEM((SIDE, SIDE, LANES, 3 * HEADS), BF16),
                pltpu.VMEM((SIDE, SIDE, REST, 3 * HEADS), BF16),
                pltpu.VMEM((PART, SEQ * LANES), BF16),
                pltpu.VMEM((PART, SEQ * REST), BF16),
                pltpu.VMEM(x_shape.shape, BF16),
                pltpu.SemaphoreType.DMA((76,)),
            ],
            outside=(2,),
            mib=20,
        )
        x = keep[0] if packed else x
        mixed, held, kv_low, kv_high = call(
            attend_kernel,
            "attend",
            (shaped(SIDE, PART, HEADS), shaped(WIDE, SEQ * HEAD_DIM), kv_shape, kv_shape),
            [SMEM, SMEM, VMEM, VMEM, VMEM] + [ANY] * 5,
            row,
            patch_order,
            q,
            exchange(kv, ALONG_X),
            small,
            o_own,
            *o_others,
            scratch=[pltpu.SemaphoreType.DMA((26,))],
            outside=(2, 3),
        )
        made = call(
            functools.partial(update_kernel, not packed),
            "update",
            (x_shape,) * packed + (parts_shape,),
            [VMEM, VMEM, ANY, ANY],
            exchange(mixed, ALONG_Z),
            held,
            x,
            mods,
            scratch=[
                pltpu.VMEM(x_shape.shape, BF16),
                pltpu.VMEM((MODS, WIDE), BF16),
                pltpu.VMEM(x_shape.shape, BF16),
                pltpu.VMEM(parts_shape.shape, BF16),
                pltpu.SemaphoreType.DMA((2,)),
            ],
            outside=(0, 1),
        )
        return *made, kv_low, kv_high

    def second_block(low, high, weights):
        spread = call(spread_kernel, "spread", shaped(SEQ, 2 * PIECE, LANES), [VMEM, VMEM], low, high)
        return later_block(None, lax.all_to_all(spread, "seq", 0, 0), *weights)

    def third_block(x, weights):
        return later_block(x, gather(x, ALONG_Z), *weights)

    early = position < 2
    one = (rows_shape, kv_shape, kv_shape)

    def not_here(*_):
        hand, *both = blank(hand_shape, *one, *one)
        return hand, [tuple(both[:3]), tuple(both[3:])]

    hand, kept = lax.cond(early, first_blocks, not_here, own, send, got, w_peer, o_peer)
    weights = lax.cond(early, no_weights, prepare, send[PACK:])
    hand, weights = lax.optimization_barrier((hand, weights))
    low = lax.ppermute(hand, "section", [(s, s + 2) for s in range(sections) if s % CHAIN == 0])
    high = lax.ppermute(hand, "section", [(s, s + 1) for s in range(sections) if s % CHAIN == 1])
    state = blank(x_shape, parts_shape, kv_shape, kv_shape)
    state = lax.cond(
        position == 2,
        lambda low, high, state, weights: second_block(low, high, weights),
        lambda low, high, state, weights: tuple(state),
        low,
        high,
        tuple(state),
        weights,
    )
    arrived = lax.ppermute(state[0], "section", [(s, s + 1) for s in range(sections) if s % CHAIN == 2])
    state = lax.cond(
        position == 3,
        lambda x, state, weights: third_block(x, weights),
        lambda x, state, weights: tuple(state),
        arrived,
        tuple(state[1:]),
        weights,
    )

    def finish_early(state, kept):
        (rows0, kv0, other0), (rows1, kv1, other1) = kept
        first = core == 0
        mine, theirs = jnp.where(first, rows0, rows1), jnp.where(first, rows1, rows0)
        other = swap(theirs)
        rows = jnp.where(first, mine, other), jnp.where(first, other, mine)
        return rows + (jnp.where(first, kv0, other1), jnp.where(first, other0, kv1))

    def finish_late(state, kept):
        parts, kv_low, kv_high = state
        rows = exchange(parts, ALONG_X)
        return rows[:, :ROWS], rows[:, ROWS:], kv_low, kv_high

    rows_low, rows_high, kv_low, kv_high = lax.cond(early, finish_early, finish_late, state, kept)
    out_t, cache = call(
        finish_kernel,
        "finish",
        (shaped(SHARD, ALL), shaped(2, ALL, HEAD_DIM)),
        [SMEM, VMEM, VMEM, VMEM, VMEM],
        patch_order,
        rows_low,
        rows_high,
        kv_low,
        kv_high,
        scratch=[pltpu.VMEM((ALL, 2 * LANES), F32)],
    )
    return jnp.transpose(out_t, (1, 0))[None], cache[None]


def solution(mesh):
    return jax.shard_map(
        body,
        mesh=mesh,
        in_specs=(
            P("section", None, "seq"),
            P(),
            P(),
            P(None, "section", None, "seq"),
            P("section", None, None, "seq"),
            P("section", None, "seq"),
            P("section", None, None, "seq"),
        ),
        out_specs=(P("section", None, "seq"), P("section", None, None, "seq")),
        check_vma=False,
    )
```

```python
import functools

import jax
import jax.numpy as jnp
from jax import lax
from jax.experimental import pallas as pl
from jax.experimental.pallas import tpu as pltpu
from jax.sharding import PartitionSpec as P

HEAD_DIM = 128
PATCHES = 8
CHAIN = 4
EPSILON = 1e-06
ROWS = 64
ALL = PATCHES * ROWS
SIDE = 4
SEQ = SIDE * SIDE
LANES = 128
REST = 64
SHARD = LANES + REST
WIDTH = SEQ * SHARD
HALF = ALL // 2
QUARTER = HALF // 2
PACK = HALF + QUARTER
PIECE = ROWS + ROWS // 2
MODS = 16
CACHE = PACK + MODS
GROUP = PATCHES // SIDE
PART = GROUP * ROWS
WIDE = SIDE * SHARD
HEADS = SIDE * HEAD_DIM
SCALE = HEAD_DIM ** (-0.5)
F32 = jnp.float32
BF16 = jnp.bfloat16
VMEM = pl.BlockSpec(memory_space=pltpu.VMEM)
SMEM = pl.BlockSpec(memory_space=pltpu.SMEM)
ANY = pl.BlockSpec(memory_space=pl.ANY)
ALONG_X = [[SIDE * i + j for i in range(SIDE)] for j in range(SIDE)]
ALONG_Z = [[SIDE * i + j for j in range(SIDE)] for i in range(SIDE)]
TRANSPOSED = (((1,), (1,)), ((), ()))


def shaped(*shape, dtype=BF16):
    return jax.ShapeDtypeStruct(shape, dtype)


def call(kernel, name, out_shape, in_specs, *args, scratch=(), mib=12, outside=()):
    many = isinstance(out_shape, tuple)
    spaces = [ANY if n in outside else VMEM for n in range(len(out_shape) if many else 1)]
    return pl.pallas_call(
        kernel,
        out_shape=out_shape,
        in_specs=in_specs,
        out_specs=tuple(spaces) if many else spaces[0],
        scratch_shapes=list(scratch),
        compiler_params=pltpu.CompilerParams(vmem_limit_bytes=mib * 1024 * 1024),
        name=name,
    )(*args)


def low_lanes(rows):
    return lax.broadcasted_iota(jnp.int32, (rows, LANES), 1) < REST


def patch_at(order_ref, j, base=0):
    return pl.ds(pl.multiple_of(base + order_ref[j] * ROWS, ROWS), ROWS)


def tile(k):
    return slice(k * LANES, (k + 1) * LANES)


def pair_lanes(low, even, odd):
    return jnp.where(low, even, pltpu.roll(odd, REST, 1))


def softmax_mix(queries, keys, values):
    scores = [
        lax.dot_general(q, k, TRANSPOSED, preferred_element_type=F32) * SCALE for q, k in zip(queries, keys, strict=True)
    ]
    tops = [jnp.max(x, axis=1, keepdims=True) for x in scores]
    terms = [jnp.exp(x - top) for x, top in zip(scores, tops, strict=True)]
    sums = [jnp.sum(x, axis=1, keepdims=True) for x in terms]
    weights = [(x * (1.0 / total)).astype(BF16) for x, total in zip(terms, sums, strict=True)]
    return [jnp.dot(w, v, preferred_element_type=F32).astype(BF16) for w, v in zip(weights, values, strict=True)]


def pack_kernel(order_ref, lat_ref, mod_ref, cache_ref, own_ref, send_ref, rows_ref):
    rows_ref[:, :SHARD] = lat_ref[...].astype(F32).T
    low = low_lanes(ROWS)
    for core, out_ref in ((0, own_ref), (1, send_ref)):
        rest = []
        for j in range(SIDE):
            at = patch_at(order_ref, core * SIDE + j)
            out_ref[j * ROWS : (j + 1) * ROWS, :] = rows_ref[at, :LANES].astype(BF16)
            rest.append(rows_ref[at, LANES:])
        for j in range(2):
            both = pair_lanes(low, rest[j], rest[j + 2])
            out_ref[HALF + j * ROWS : HALF + (j + 1) * ROWS, :] = both.astype(BF16)
    mod = mod_ref[...]
    lines = []
    for kind in (1.0 + mod[1:2], mod[0:1], mod[2:3]):
        last = jnp.concatenate([kind[:, LANES:], kind[:, LANES:]], axis=1)
        for value in (kind[:, :LANES], last):
            high = value.astype(BF16).astype(F32)
            lines += [high, value - high]
    lines.append(jnp.zeros((MODS - len(lines), LANES), F32))
    send_ref[PACK : PACK + MODS, :] = jnp.concatenate(lines, axis=0).astype(BF16)
    for part in range(2):
        send_ref[CACHE + part * ALL : CACHE + (part + 1) * ALL, :] = cache_ref[part]


def mods_of(flag_ref, t, send_ref, got_ref):
    return jnp.where(flag_ref[t] == 1, send_ref[PACK:CACHE, :], got_ref[PACK:CACHE, :])


def start_kernel(flag_ref, own_ref, send_ref, got_ref, x_ref, out_ref):
    x = jnp.where(flag_ref[2] == 0, own_ref[...], got_ref[:PACK, :])
    mods = mods_of(flag_ref, 0, send_ref, got_ref)
    x_ref[...] = x
    for s in range(SIDE):
        out_ref[s, :PACK, :] = x
        out_ref[s, PACK:, :] = mods


def place(flag_ref, s):
    return jnp.where(flag_ref[2] == 0, s, (s % SIDE) * SIDE + s // SIDE)


def project_half_kernel(t_now, flag_ref, x_ref, own_ref, peer_ref, q_ref, kv_ref, wm_ref, wr_ref, nm_ref, nr_ref, sems):
    def copies(w_ref):
        found = []
        for t in range(3):
            lanes = pl.ds(t * HEAD_DIM, HEAD_DIM)
            found.append(pltpu.make_async_copy(w_ref.at[t, :, :LANES, :], wm_ref.at[:, :, lanes], sems.at[2 * t]))
            found.append(pltpu.make_async_copy(w_ref.at[t, :, LANES:, :], wr_ref.at[:, :, lanes], sems.at[2 * t + 1]))
        return found

    @pl.when(flag_ref[t_now] == 1)
    def _():
        for copy in copies(own_ref):
            copy.start()

    @pl.when(flag_ref[t_now] == 0)
    def _():
        for copy in copies(peer_ref):
            copy.start()

    low = low_lanes(ROWS)
    at = [place(flag_ref, s) for s in range(SEQ)]

    def line(s, k):
        pair = x_ref[at[s], PACK:, :].astype(F32)
        return pair[2 * k : 2 * k + 1] + pair[2 * k + 1 : 2 * k + 2]

    scale_first = [line(s, 0) for s in range(SEQ)]
    shift_first = [line(s, 2) for s in range(SEQ)]
    scale_last = [jnp.where(low[:1], line(2 * p, 1), line(2 * p + 1, 1)) for p in range(SEQ // 2)]
    shift_last = [jnp.where(low[:1], line(2 * p, 3), line(2 * p + 1, 3)) for p in range(SEQ // 2)]
    for j in range(SIDE):
        mine = pl.ds(j * ROWS, ROWS)
        rest = pl.ds(HALF + (j % 2) * ROWS, ROWS)
        total = jnp.zeros((ROWS, LANES), F32)
        square = jnp.zeros((ROWS, LANES), F32)
        total_rest = jnp.zeros((ROWS, LANES), F32)
        square_rest = jnp.zeros((ROWS, LANES), F32)
        for s in range(SEQ):
            x = x_ref[at[s], mine, :].astype(F32)
            total = total + x
            square = square + x * x
            x = x_ref[at[s], rest, :].astype(F32)
            total_rest = total_rest + x
            square_rest = square_rest + x * x
        in_half = low if j < 2 else jnp.logical_not(low)
        total = total + jnp.where(in_half, total_rest, 0.0)
        square = square + jnp.where(in_half, square_rest, 0.0)
        mean = jnp.sum(total, axis=1, keepdims=True) / WIDTH
        var = jnp.sum(square, axis=1, keepdims=True) / WIDTH - mean * mean
        rstd = lax.rsqrt(var + EPSILON)
        for s in range(SEQ):
            x = x_ref[at[s], mine, :].astype(F32)
            normed = (x - mean) * rstd * scale_first[s] + shift_first[s]
            nm_ref[mine, tile(s)] = normed.astype(BF16)
        for p in range(SEQ // 2):
            even = x_ref[at[2 * p], rest, :].astype(F32)
            odd = x_ref[at[2 * p + 1], rest, :].astype(F32)
            if j < 2:
                x = pair_lanes(low, even, odd)
            else:
                x = jnp.where(low, pltpu.roll(even, REST, 1), odd)
            normed = (x - mean) * rstd * scale_last[p] + shift_last[p]
            nr_ref[mine, tile(p)] = normed.astype(BF16)

    for copy in copies(own_ref):
        copy.wait()
    w_first = wm_ref[...].reshape(SEQ * LANES, 3 * HEAD_DIM)
    w_last = wr_ref[...].reshape(SEQ * REST, 3 * HEAD_DIM)
    qkv = jnp.dot(nm_ref[...], w_first, preferred_element_type=F32)
    qkv = qkv + jnp.dot(nr_ref[...], w_last, preferred_element_type=F32)
    qkv = qkv.astype(BF16)
    q_ref[...] = qkv[:, :HEAD_DIM]
    kv_ref[0] = qkv[:, HEAD_DIM : 2 * HEAD_DIM]
    kv_ref[1] = qkv[:, 2 * HEAD_DIM :]


def attend_half_kernel(t, flag_ref, order_ref, q_ref, kv_ref, other_ref, own_ref, got_ref, *refs):
    o_own_ref, o_peer_ref, out_ref, w_ref, kv_out_ref, other_out_ref, sem, sems = refs
    leaving = [pltpu.make_async_copy(kv_ref, kv_out_ref, sems.at[0])]
    leaving.append(pltpu.make_async_copy(other_ref, other_out_ref, sems.at[1]))
    for copy in leaving:
        copy.start()

    @pl.when(flag_ref[t] == 1)
    def _():
        pltpu.make_async_copy(o_own_ref, w_ref, sem).start()

    @pl.when(flag_ref[t] == 0)
    def _():
        pltpu.make_async_copy(o_peer_ref, w_ref, sem).start()

    mine = flag_ref[t] == 1
    core = flag_ref[2]

    def stale(part, j):
        peer = got_ref[patch_at(order_ref, j, CACHE + part * ALL), :]
        return jnp.where(mine, own_ref[part, patch_at(order_ref, j), :], peer)

    old, other = [], []
    for part in range(2):
        old.append([stale(part, core * SIDE + j) for j in range(SIDE)])
        kept = jnp.concatenate([stale(part, (1 - core) * SIDE + j) for j in range(SIDE)], axis=0)
        other.append(jnp.where(core == 1, other_ref[part], kept))
    queries, keys, values = [], [], []
    for j in range(SIDE):
        queries.append(q_ref[j * ROWS : (j + 1) * ROWS, :])
        for part, found in ((0, keys), (1, values)):
            parts = [kv_ref[part, : (j + 1) * ROWS, :]] + old[part][j + 1 :] + [other[part]]
            found.append(jnp.concatenate(parts, axis=0))
    for j, mixed in enumerate(softmax_mix(queries, keys, values)):
        for s in range(SIDE):
            out_ref[s, j * ROWS : (j + 1) * ROWS, :] = mixed
    pltpu.make_async_copy(o_own_ref, w_ref, sem).wait()
    for copy in leaving:
        copy.wait()


def update_half_kernel(t, flag_ref, mixed_ref, w_ref, x_ref, send_ref, got_ref, rows_out_ref, *refs):
    last = t == 1
    if last:
        hand_out_ref, held_ref, rows_ref, hand_ref, sems = refs
    else:
        new_ref, spread_ref, held_ref, rows_ref, _, sems = refs

    mixed = jnp.concatenate([mixed_ref[place(flag_ref, h)] for h in range(SEQ)], axis=1)
    held_ref[:, :SHARD] = lax.dot_general(mixed, w_ref[...], TRANSPOSED, preferred_element_type=F32)
    mods = mods_of(flag_ref, t, send_ref, got_ref).astype(F32)
    gate_first = mods[8:9] + mods[9:10]
    gate_last = mods[10:11] + mods[11:12]
    first = (x_ref[:HALF, :].astype(F32) + gate_first * held_ref[:, :LANES]).astype(BF16)
    made = pair_lanes(low_lanes(QUARTER), held_ref[:QUARTER, LANES:], held_ref[QUARTER:, LANES:])
    rest = x_ref[HALF:, :].astype(F32) + gate_last * made
    other = pltpu.roll(rest, REST, 1)
    if last:
        for n in range(SIDE):
            lines = (rest if n < 2 else other)[(n % 2) * ROWS : (n % 2 + 1) * ROWS]
            hand_ref[n, :ROWS, :] = first[n * ROWS : (n + 1) * ROWS]
            both = pair_lanes(low_lanes(ROWS // 2), lines[: ROWS // 2], lines[ROWS // 2 :])
            hand_ref[n, ROWS:, :] = both.astype(BF16)
        out = [pltpu.make_async_copy(hand_ref, hand_out_ref, sems.at[1])]
        out[0].start()
    else:
        out = []
    other = other.astype(BF16)
    rest = rest.astype(BF16)
    for n in range(SIDE):
        at = slice((n % 2) * ROWS, (n % 2 + 1) * ROWS)
        rows_ref[n, :, :LANES] = first[n * ROWS : (n + 1) * ROWS]
        rows_ref[n, :, LANES:] = rest[at] if n < 2 else other[at]
    out.append(pltpu.make_async_copy(rows_ref, rows_out_ref, sems.at[0]))
    out[-1].start()
    if not last:
        mods = mods_of(flag_ref, 1, send_ref, got_ref)
        new_ref[:HALF, :] = first
        new_ref[HALF:, :] = rest
        for s in range(SIDE):
            spread_ref[s, :HALF, :] = first
            spread_ref[s, HALF:PACK, :] = rest
            spread_ref[s, PACK:, :] = mods
    for copy in out:
        copy.wait()


def mods_kernel(gathered_ref, out_ref):
    low = low_lanes(1)
    rows = [gathered_ref[i, :MODS, :].astype(F32) for i in range(SIDE)]
    lines = []
    for k in range(3):
        for h in range(2):
            first, last = 4 * k + h, 4 * k + 2 + h
            parts = [rows[i][first : first + 1] for i in range(SIDE)]
            for m in range(SIDE // 2):
                even, odd = (rows[2 * m + e][last : last + 1] for e in range(2))
                parts.append(jnp.where(low, even, odd))
            lines.append(jnp.concatenate(parts, axis=1))
    lines.append(jnp.zeros((MODS - len(lines), WIDE), F32))
    out_ref[...] = jnp.concatenate(lines, axis=0).astype(BF16)


def spread_kernel(low_ref, high_ref, out_ref):
    for s in range(SEQ):
        out_ref[s, :PIECE, :] = low_ref[s // SIDE]
        out_ref[s, PIECE:, :] = high_ref[s // SIDE]


def unpack(even, odd):
    low = low_lanes(ROWS // 2)
    return jnp.concatenate([pair_lanes(low, even, odd), jnp.where(low, pltpu.roll(even, REST, 1), odd)], axis=0)


def project_kernel(packed, row_ref, x_ref, mods_in_ref, w_ref, below_ref, above_ref, *refs):
    across_low_ref, across_high_ref, q_ref, kv_ref, *refs = refs
    if packed:
        keep_out_ref, *refs = refs
    wm_ref, wr_ref, nm_ref, nr_ref, keep_ref, mods_ref, sems = refs
    mods_copy = pltpu.make_async_copy(mods_in_ref, mods_ref, sems.at[76])
    mods_copy.start()
    i = row_ref[0]
    half = SIDE // 2
    sources = (
        (w_ref, 0, SIDE, i),
        (below_ref, 0, SIDE, lax.rem(i + 3, SIDE)),
        (above_ref, 0, SIDE, lax.rem(i + 1, SIDE)),
        (across_low_ref, 0, half, lax.rem(i + 2, SIDE)),
        (across_high_ref, half, SIDE, lax.rem(i + 2, SIDE)),
    )
    copies = []
    for t in range(3):
        for source, first, last, h in sources:
            lanes = pl.ds(pl.multiple_of((t * SIDE + h) * HEAD_DIM, HEAD_DIM), HEAD_DIM)
            pairs = [(source.at[t, :, :, :LANES, :], wm_ref.at[first:last, :, :, lanes])]
            pairs += [(source.at[t, :, j, LANES:, :], wr_ref.at[j, first:last, :, lanes]) for j in range(SIDE)]
            copies += [pltpu.make_async_copy(a, b, sems.at[len(copies) + n]) for n, (a, b) in enumerate(pairs)]
    for copy in copies:
        copy.start()
    mods_copy.wait()
    mods = [mods_ref[j].astype(F32) for j in range(SIDE)]
    scale = [m[0:1] + m[1:2] for m in mods]
    shift = [m[2:3] + m[3:4] for m in mods]
    tiles = WIDE // LANES

    def features(g, j, k):
        if not packed:
            return x_ref[j, g * ROWS : (g + 1) * ROWS, tile(k)].astype(F32)
        if k < SIDE:
            return x_ref[k * SIDE + j, g * PIECE : g * PIECE + ROWS, :].astype(F32)
        pair = (2 * (k - SIDE) * SIDE + j, (2 * (k - SIDE) + 1) * SIDE + j)
        return unpack(*(x_ref[s, g * PIECE + ROWS : (g + 1) * PIECE, :].astype(F32) for s in pair))

    for g in range(GROUP):
        mine = pl.ds(g * ROWS, ROWS)
        total, square = (jnp.zeros((ROWS, LANES), F32) for _ in range(2))
        for j in range(SIDE):
            for k in range(tiles):
                x = features(g, j, k)
                total = total + x
                square = square + x * x
        mean = jnp.sum(total, axis=1, keepdims=True) / WIDTH
        var = jnp.sum(square, axis=1, keepdims=True) / WIDTH - mean * mean
        rstd = lax.rsqrt(var + EPSILON)
        for j in range(SIDE):
            for k in range(tiles):
                x = features(g, j, k)
                normed = ((x - mean) * rstd * scale[j][:, tile(k)] + shift[j][:, tile(k)]).astype(BF16)
                if k < SIDE:
                    nm_ref[mine, tile(k * SIDE + j)] = normed
                else:
                    nr_ref[mine, tile(j * (SIDE // 2) + k - SIDE)] = normed
        if packed:
            for k in range(tiles):
                keep_ref[mine, tile(k)] = features(g, row_ref[1], k).astype(BF16)
    kept = [pltpu.make_async_copy(keep_ref, keep_out_ref, sems.at[len(copies)])] if packed else []
    for copy in kept:
        copy.start()
    each = len(copies) // 3
    for t in range(3):
        for copy in copies[t * each : (t + 1) * each]:
            copy.wait()
        lanes = slice(t * HEADS, (t + 1) * HEADS)
        part = jnp.dot(nm_ref[...], wm_ref[:, :, :, lanes].reshape(SEQ * LANES, HEADS), preferred_element_type=F32)
        part = part + jnp.dot(nr_ref[...], wr_ref[:, :, :, lanes].reshape(SEQ * REST, HEADS), preferred_element_type=F32)
        part = part.astype(BF16)
        if t == 0:
            q_ref[...] = part
        else:
            for s in range(SIDE):
                kv_ref[s, :, (t - 1) * HEADS : t * HEADS] = part
    for copy in kept:
        copy.wait()


def load_out(i, w_ref, below_ref, above_ref, across_low_ref, across_high_ref, held_ref, sems):
    width = SEQ * HEAD_DIM
    sources = (
        (w_ref, 0, width, i),
        (below_ref, 0, width, lax.rem(i + 3, SIDE)),
        (above_ref, 0, width, lax.rem(i + 1, SIDE)),
        (across_low_ref, 0, width // 2, lax.rem(i + 2, SIDE)),
        (across_high_ref, width // 2, width, lax.rem(i + 2, SIDE)),
    )
    copies = []
    for source, begin, end, h in sources:
        first = pl.ds(pl.multiple_of(h * LANES, LANES), LANES)
        last = pl.ds(pl.multiple_of(SIDE * LANES + h * REST, REST), REST)
        for taken, rows in ((slice(0, LANES), first), (slice(LANES, SHARD), last)):
            held = held_ref.at[rows, begin:end]
            copies.append(pltpu.make_async_copy(source.at[taken, :], held, sems.at[len(copies)]))
    return copies


def attend_kernel(row_ref, order_ref, q_ref, kv_ref, stale_ref, *refs):
    *w_refs, out_ref, held_ref, low_ref, high_ref, sems = refs
    i = row_ref[0]
    copies = load_out(i, *w_refs, held_ref, sems)
    for part in range(2):
        lanes = pl.ds(pl.multiple_of(part * HEADS + i * HEAD_DIM, HEAD_DIM), HEAD_DIM)
        for n in range(SIDE):
            for half, own_ref in enumerate((low_ref, high_ref)):
                new = kv_ref.at[n, half * ROWS : (half + 1) * ROWS, lanes]
                own = own_ref.at[part, n * ROWS : (n + 1) * ROWS, :]
                copies.append(pltpu.make_async_copy(new, own, sems.at[len(copies)]))
    for copy in copies:
        copy.start()
    for pair in range(SIDE // 2):
        where, queries, keys, values = [], [], [], []
        for h in (2 * pair, 2 * pair + 1):
            new, old = [], []
            for part in range(2):
                lanes = tile(part * SIDE + h)
                halves = [slice(g * ROWS, (g + 1) * ROWS) for g in range(GROUP)]
                new.append([kv_ref[n % SIDE, halves[n // SIDE], lanes] for n in range(PATCHES)])
                old.append([stale_ref[h, patch_at(order_ref, n, MODS + part * ALL), :] for n in range(PATCHES)])
            for g in range(GROUP):
                where.append((halves[g], tile(h)))
                queries.append(q_ref[halves[g], tile(h)])
                for part, found in ((0, keys), (1, values)):
                    rows = [jnp.where(n <= i + SIDE * g, new[part][n], old[part][n]) for n in range(PATCHES)]
                    found.append(jnp.concatenate(rows, axis=0))
        for (rows, lanes), mixed in zip(where, softmax_mix(queries, keys, values), strict=True):
            for s in range(SIDE):
                out_ref[s, rows, lanes] = mixed
    for copy in copies:
        copy.wait()


def update_kernel(last, mixed_ref, held_ref, x_in_ref, mods_in_ref, *refs):
    if not last:
        out_ref, *refs = refs
    part_ref, x_ref, mods_ref, made_ref, cut_ref, sems = refs
    copies = []
    copies.append(pltpu.make_async_copy(x_in_ref, x_ref, sems.at[len(copies)]))
    copies.append(pltpu.make_async_copy(mods_in_ref, mods_ref, sems.at[len(copies)]))
    for copy in copies:
        copy.start()
    mixed = jnp.concatenate([mixed_ref[h % SIDE, :, tile(h // SIDE)] for h in range(SEQ)], axis=1)
    for copy in copies:
        copy.wait()
    made = lax.dot_general(mixed, held_ref[...], TRANSPOSED, preferred_element_type=F32)
    mods = mods_ref[...].astype(F32)
    new = x_ref[...].astype(F32) + (mods[4:5] + mods[5:6]) * made
    out = []
    if not last:
        made_ref[...] = new.astype(BF16)
        out.append(pltpu.make_async_copy(made_ref, out_ref, sems.at[0]))
        out[0].start()
    for n in range(SIDE):
        rest = new[:, tile(SIDE + n // 2)]
        cut_ref[n, :, :LANES] = new[:, tile(n)].astype(BF16)
        cut_ref[n, :, LANES:] = (rest if n % 2 == 0 else pltpu.roll(rest, REST, 1)).astype(BF16)
    out.append(pltpu.make_async_copy(cut_ref, part_ref, sems.at[1]))
    out[-1].start()
    for copy in out:
        copy.wait()


def finish_kernel(order_ref, low_ref, high_ref, kv_low_ref, kv_high_ref, out_ref, cache_ref, rows_ref):
    for half, (x_ref, kv_ref) in enumerate(((low_ref, kv_low_ref), (high_ref, kv_high_ref))):
        for n in range(SIDE):
            at = patch_at(order_ref, half * SIDE + n)
            rows_ref[at, :] = x_ref[n].astype(F32)
            for part in range(2):
                cache_ref[part, at, :] = kv_ref[part, n * ROWS : (n + 1) * ROWS, :]
    out_ref[...] = rows_ref[...].T[:SHARD, :].astype(BF16)


def blank(*shapes):
    return pl.pallas_call(lambda *refs: None, out_shape=shapes, out_specs=(ANY,) * len(shapes), name="blank")()


def body(latents, patch_order, timestep, mod_table, w_qkv, w_out, kv_cache):
    sections = lax.axis_size("section")
    section = lax.axis_index("section")
    position = section % CHAIN
    core = (section % 2).astype(jnp.int32)
    seq = lax.axis_index("seq").astype(jnp.int32)
    row = jnp.stack([seq // SIDE, seq % SIDE])
    w_own = jnp.transpose(w_qkv[0], (1, 0, 2))
    o_own = jnp.transpose(w_out[0], (1, 0))
    cache_own = kv_cache[0]
    mod_now = lax.dynamic_index_in_dim(mod_table, timestep[0], 0, keepdims=False)[0]

    def swap(value):
        return lax.ppermute(value, "section", [(s, s ^ 1) for s in range(sections) if s % CHAIN < 2])

    def exchange(value, groups):
        return lax.all_to_all(value, "seq", 0, 0, axis_index_groups=groups)

    def shift(value, by):
        pairs = [(s, (s + SIDE * by) % SEQ) for s in range(SEQ)]
        return lax.ppermute(value, "seq", pairs)

    def by_core(value, even, odd):
        groups = [[s * SEQ + d for d in g] for s in range(sections) for g in (odd if s % 2 else even)]
        return lax.all_to_all(value, ("section", "seq"), 0, 0, axis_index_groups=groups)

    def gather_mixed(spread):
        near = by_core(spread, ALONG_Z, ALONG_X)
        far = by_core(jnp.broadcast_to(near[None], (SIDE,) + near.shape), ALONG_X, ALONG_Z)
        return far.reshape((SEQ,) + near.shape[1:])

    def gather(value, groups):
        return exchange(jnp.broadcast_to(value[None], (SIDE,) + value.shape), groups)

    rows_shape, kv_shape = shaped(SIDE, ROWS, 2 * LANES), shaped(2, HALF, HEAD_DIM)
    hand_shape, x_shape, parts_shape = shaped(SIDE, PIECE, LANES), shaped(PART, WIDE), shaped(SIDE, PART, 2 * LANES)

    flags = jnp.stack([core == 0, core == 1, core]).astype(jnp.int32)
    flags, mod_now = lax.optimization_barrier((flags, mod_now))
    own, send = call(
        pack_kernel,
        "pack",
        (shaped(PACK, LANES), shaped(CACHE + 2 * ALL, LANES)),
        [SMEM, VMEM, VMEM, VMEM],
        patch_order,
        jnp.transpose(latents[0], (1, 0)),
        mod_now,
        cache_own,
        scratch=[pltpu.VMEM((ALL, 2 * LANES), F32)],
    )
    own, send, w_own, o_own = lax.optimization_barrier((own, send, w_own, o_own))
    got, w_peer, o_peer = swap(send), swap(w_own), swap(o_own)
    got, w_peer, o_peer = lax.optimization_barrier((got, w_peer, o_peer))

    spread_shape = shaped(SIDE, PACK + MODS, LANES)

    def first_blocks(own, send, got, w_peer, o_peer):
        shapes = shaped(PACK, LANES), spread_shape
        x, spread = call(start_kernel, "start", shapes, [SMEM, VMEM, VMEM, VMEM], flags, own, send, got)
        gathered = gather_mixed(spread)
        kept = []
        for t in range(2):
            q, kv = call(
                functools.partial(project_half_kernel, t),
                "project_half",
                (shaped(HALF, HEAD_DIM), kv_shape),
                [SMEM, VMEM, ANY, ANY],
                flags,
                gathered,
                w_own.reshape(3, SEQ, SHARD, HEAD_DIM),
                w_peer.reshape(3, SEQ, SHARD, HEAD_DIM),
                scratch=[
                    pltpu.VMEM((SEQ, LANES, 3 * HEAD_DIM), BF16),
                    pltpu.VMEM((SEQ, REST, 3 * HEAD_DIM), BF16),
                    pltpu.VMEM((HALF, SEQ * LANES), BF16),
                    pltpu.VMEM((HALF, SEQ * REST), BF16),
                    pltpu.SemaphoreType.DMA((6,)),
                ],
            )
            kv_other = swap(kv)
            mixed, w_now, kv_kept, other_kept = call(
                functools.partial(attend_half_kernel, t),
                "attend_half",
                (shaped(SIDE, HALF, HEAD_DIM), shaped(*o_own.shape), kv_shape, kv_shape),
                [SMEM, SMEM, VMEM, VMEM, VMEM, VMEM, VMEM, ANY, ANY],
                flags,
                patch_order,
                q,
                kv,
                kv_other,
                cache_own,
                got,
                o_own,
                o_peer,
                scratch=[pltpu.SemaphoreType.DMA, pltpu.SemaphoreType.DMA((2,))],
                outside=(2, 3),
            )
            heads = gather_mixed(mixed)
            last = t == 1
            results = call(
                functools.partial(update_half_kernel, t),
                "update_half",
                (rows_shape,) + ((hand_shape,) if last else (shaped(PACK, LANES), spread_shape)),
                [SMEM, VMEM, VMEM, VMEM, VMEM, VMEM],
                flags,
                heads,
                w_now,
                x,
                send,
                got,
                scratch=[
                    pltpu.VMEM((HALF, 2 * LANES), F32),
                    pltpu.VMEM(rows_shape.shape, BF16),
                    pltpu.VMEM(hand_shape.shape, BF16),
                    pltpu.SemaphoreType.DMA((2,)),
                ],
                outside=(0, 1) if last else (0,),
            )
            if not last:
                x, gathered = results[1], gather_mixed(results[2])
            kept.append((results[0], kv_kept, other_kept))
        return results[1], kept

    half_width = SEQ * HEAD_DIM // 2

    def prepare(small):
        w = w_own.reshape(3, SIDE, SIDE, SHARD, HEAD_DIM)
        w_near, o, small = lax.optimization_barrier(((shift(w, 1), shift(w, -1)), o_own, small))
        w_far = shift(w_near[0][:, : SIDE // 2], 1), shift(w_near[1][:, SIDE // 2 :], -1)
        o_near = shift(o, 1), shift(o, -1)
        small = gather(small, ALONG_X)
        mods = call(mods_kernel, "mods", shaped(MODS, WIDE), [VMEM], small, mib=4)
        others = gather(mods, ALONG_Z), small, mods
        w_far, o_near, others = lax.optimization_barrier((w_far, o_near, others))
        o_far = shift(o_near[0][:, :half_width], 1), shift(o_near[1][:, half_width:], -1)
        mods_all, small, mods = others
        return w_near + w_far, o_near + o_far, small, mods, mods_all

    def no_weights(small):
        side, half = (shaped(3, n, SIDE, SHARD, HEAD_DIM) for n in (SIDE, SIDE // 2))
        whole, part = (shaped(SHARD, n) for n in (2 * half_width, half_width))
        shapes = (side, side, half, half, whole, whole, part, part)
        shapes += (shaped(SIDE, *small.shape), shaped(MODS, WIDE), shaped(SIDE, MODS, WIDE))
        made = blank(*shapes)
        return tuple(made[:4]), tuple(made[4:8]), *made[8:]

    def later_block(x, gathered, w_others, o_others, small, mods, mods_all):
        packed = x is None
        q, kv, *keep = call(
            functools.partial(project_kernel, packed),
            "project",
            (shaped(PART, HEADS), shaped(SIDE, PART, 2 * HEADS)) + (x_shape,) * packed,
            [SMEM, VMEM] + [ANY] * 6,
            row,
            gathered,
            mods_all,
            w_own.reshape(3, SIDE, SIDE, SHARD, HEAD_DIM),
            *w_others,
            scratch=[
                pltpu.VMEM((SIDE, SIDE, LANES, 3 * HEADS), BF16),
                pltpu.VMEM((SIDE, SIDE, REST, 3 * HEADS), BF16),
                pltpu.VMEM((PART, SEQ * LANES), BF16),
                pltpu.VMEM((PART, SEQ * REST), BF16),
                pltpu.VMEM(x_shape.shape, BF16),
                pltpu.VMEM((SIDE, MODS, WIDE), BF16),
                pltpu.SemaphoreType.DMA((77,)),
            ],
            outside=(2,),
            mib=20,
        )
        x = keep[0] if packed else x
        mixed, held, kv_low, kv_high = call(
            attend_kernel,
            "attend",
            (shaped(SIDE, PART, HEADS), shaped(WIDE, SEQ * HEAD_DIM), kv_shape, kv_shape),
            [SMEM, SMEM, VMEM, VMEM, VMEM] + [ANY] * 5,
            row,
            patch_order,
            q,
            exchange(kv, ALONG_X),
            small,
            o_own,
            *o_others,
            scratch=[pltpu.SemaphoreType.DMA((26,))],
            outside=(2, 3),
        )
        made = call(
            functools.partial(update_kernel, not packed),
            "update",
            (x_shape,) * packed + (parts_shape,),
            [VMEM, VMEM, ANY, ANY],
            exchange(mixed, ALONG_Z),
            held,
            x,
            mods,
            scratch=[
                pltpu.VMEM(x_shape.shape, BF16),
                pltpu.VMEM((MODS, WIDE), BF16),
                pltpu.VMEM(x_shape.shape, BF16),
                pltpu.VMEM(parts_shape.shape, BF16),
                pltpu.SemaphoreType.DMA((2,)),
            ],
            outside=(0, 1),
        )
        return *made, kv_low, kv_high

    def second_block(low, high, weights):
        spread = call(spread_kernel, "spread", shaped(SEQ, 2 * PIECE, LANES), [VMEM, VMEM], low, high)
        return later_block(None, lax.all_to_all(spread, "seq", 0, 0), *weights)

    def third_block(x, weights):
        return later_block(x, gather(x, ALONG_Z), *weights)

    early = position < 2
    one = (rows_shape, kv_shape, kv_shape)

    def not_here(*_):
        hand, *both = blank(hand_shape, *one, *one)
        return hand, [tuple(both[:3]), tuple(both[3:])]

    hand, kept = lax.cond(early, first_blocks, not_here, own, send, got, w_peer, o_peer)
    weights = lax.cond(early, no_weights, prepare, send[PACK:])
    hand, weights = lax.optimization_barrier((hand, weights))
    low = lax.ppermute(hand, "section", [(s, s + 2) for s in range(sections) if s % CHAIN == 0])
    high = lax.ppermute(hand, "section", [(s, s + 1) for s in range(sections) if s % CHAIN == 1])
    state = blank(x_shape, parts_shape, kv_shape, kv_shape)
    state = lax.cond(
        position == 2,
        lambda low, high, state, weights: second_block(low, high, weights),
        lambda low, high, state, weights: tuple(state),
        low,
        high,
        tuple(state),
        weights,
    )
    arrived = lax.ppermute(state[0], "section", [(s, s + 1) for s in range(sections) if s % CHAIN == 2])
    state = lax.cond(
        position == 3,
        lambda x, state, weights: third_block(x, weights),
        lambda x, state, weights: tuple(state),
        arrived,
        tuple(state[1:]),
        weights,
    )

    def finish_early(state, kept):
        (rows0, kv0, other0), (rows1, kv1, other1) = kept
        first = core == 0
        mine, theirs = jnp.where(first, rows0, rows1), jnp.where(first, rows1, rows0)
        other = swap(theirs)
        rows = jnp.where(first, mine, other), jnp.where(first, other, mine)
        return rows + (jnp.where(first, kv0, other1), jnp.where(first, other0, kv1))

    def finish_late(state, kept):
        parts, kv_low, kv_high = state
        rows = exchange(parts, ALONG_X)
        return rows[:, :ROWS], rows[:, ROWS:], kv_low, kv_high

    rows_low, rows_high, kv_low, kv_high = lax.cond(early, finish_early, finish_late, state, kept)
    out_t, cache = call(
        finish_kernel,
        "finish",
        (shaped(SHARD, ALL), shaped(2, ALL, HEAD_DIM)),
        [SMEM, VMEM, VMEM, VMEM, VMEM],
        patch_order,
        rows_low,
        rows_high,
        kv_low,
        kv_high,
        scratch=[pltpu.VMEM((ALL, 2 * LANES), F32)],
    )
    return jnp.transpose(out_t, (1, 0))[None], cache[None]


def solution(mesh):
    return jax.shard_map(
        body,
        mesh=mesh,
        in_specs=(
            P("section", None, "seq"),
            P(),
            P(),
            P(None, "section", None, "seq"),
            P("section", None, None, "seq"),
            P("section", None, "seq"),
            P("section", None, None, "seq"),
        ),
        out_specs=(P("section", None, "seq"), P("section", None, None, "seq")),
        check_vma=False,
    )
```

```python
import functools

import jax
import jax.numpy as jnp
from jax import lax
from jax.experimental import pallas as pl
from jax.experimental.pallas import tpu as pltpu
from jax.sharding import PartitionSpec as P

HEAD_DIM = 128
PATCHES = 8
CHAIN = 4
EPSILON = 1e-06
ROWS = 64
ALL = PATCHES * ROWS
SIDE = 4
SEQ = SIDE * SIDE
LANES = 128
REST = 64
SHARD = LANES + REST
WIDTH = SEQ * SHARD
HALF = ALL // 2
QUARTER = HALF // 2
PACK = HALF + QUARTER
PIECE = ROWS + ROWS // 2
MODS = 16
CACHE = PACK + MODS
GROUP = PATCHES // SIDE
PART = GROUP * ROWS
WIDE = SIDE * SHARD
HEADS = SIDE * HEAD_DIM
SCALE = HEAD_DIM ** (-0.5)
F32 = jnp.float32
BF16 = jnp.bfloat16
VMEM = pl.BlockSpec(memory_space=pltpu.VMEM)
SMEM = pl.BlockSpec(memory_space=pltpu.SMEM)
ANY = pl.BlockSpec(memory_space=pl.ANY)
ALONG_X = [[SIDE * i + j for i in range(SIDE)] for j in range(SIDE)]
ALONG_Z = [[SIDE * i + j for j in range(SIDE)] for i in range(SIDE)]
TRANSPOSED = (((1,), (1,)), ((), ()))


def shaped(*shape, dtype=BF16):
    return jax.ShapeDtypeStruct(shape, dtype)


def call(kernel, name, out_shape, in_specs, *args, scratch=(), mib=12, outside=()):
    many = isinstance(out_shape, tuple)
    spaces = [ANY if n in outside else VMEM for n in range(len(out_shape) if many else 1)]
    return pl.pallas_call(
        kernel,
        out_shape=out_shape,
        in_specs=in_specs,
        out_specs=tuple(spaces) if many else spaces[0],
        scratch_shapes=list(scratch),
        compiler_params=pltpu.CompilerParams(vmem_limit_bytes=mib * 1024 * 1024),
        name=name,
    )(*args)


def low_lanes(rows):
    return lax.broadcasted_iota(jnp.int32, (rows, LANES), 1) < REST


def patch_at(order_ref, j, base=0):
    return pl.ds(pl.multiple_of(base + order_ref[j] * ROWS, ROWS), ROWS)


def tile(k):
    return slice(k * LANES, (k + 1) * LANES)


def pair_lanes(low, even, odd):
    return jnp.where(low, even, pltpu.roll(odd, REST, 1))


def softmax_mix(queries, keys, values):
    scores = [
        lax.dot_general(q, k, TRANSPOSED, preferred_element_type=F32) * SCALE for q, k in zip(queries, keys, strict=True)
    ]
    tops = [jnp.max(x, axis=1, keepdims=True) for x in scores]
    terms = [jnp.exp(x - top) for x, top in zip(scores, tops, strict=True)]
    sums = [jnp.sum(x, axis=1, keepdims=True) for x in terms]
    weights = [(x * (1.0 / total)).astype(BF16) for x, total in zip(terms, sums, strict=True)]
    return [jnp.dot(w, v, preferred_element_type=F32).astype(BF16) for w, v in zip(weights, values, strict=True)]


def pack_kernel(order_ref, lat_ref, mod_ref, cache_ref, own_ref, send_ref, rows_ref):
    rows_ref[:, :SHARD] = lat_ref[...].astype(F32).T
    low = low_lanes(ROWS)
    for core, out_ref in ((0, own_ref), (1, send_ref)):
        rest = []
        for j in range(SIDE):
            at = patch_at(order_ref, core * SIDE + j)
            out_ref[j * ROWS : (j + 1) * ROWS, :] = rows_ref[at, :LANES].astype(BF16)
            rest.append(rows_ref[at, LANES:])
        for j in range(2):
            both = pair_lanes(low, rest[j], rest[j + 2])
            out_ref[HALF + j * ROWS : HALF + (j + 1) * ROWS, :] = both.astype(BF16)
    mod = mod_ref[...]
    lines = []
    for kind in (1.0 + mod[1:2], mod[0:1], mod[2:3]):
        last = jnp.concatenate([kind[:, LANES:], kind[:, LANES:]], axis=1)
        for value in (kind[:, :LANES], last):
            high = value.astype(BF16).astype(F32)
            lines += [high, value - high]
    lines.append(jnp.zeros((MODS - len(lines), LANES), F32))
    send_ref[PACK : PACK + MODS, :] = jnp.concatenate(lines, axis=0).astype(BF16)
    for part in range(2):
        send_ref[CACHE + part * ALL : CACHE + (part + 1) * ALL, :] = cache_ref[part]


def mods_of(flag_ref, t, send_ref, got_ref):
    return jnp.where(flag_ref[t] == 1, send_ref[PACK:CACHE, :], got_ref[PACK:CACHE, :])


def start_kernel(flag_ref, own_ref, send_ref, got_ref, x_ref, out_ref):
    x = jnp.where(flag_ref[2] == 0, own_ref[...], got_ref[:PACK, :])
    mods = mods_of(flag_ref, 0, send_ref, got_ref)
    x_ref[...] = x
    for s in range(SIDE):
        out_ref[s, :PACK, :] = x
        out_ref[s, PACK:, :] = mods


def place(flag_ref, s):
    return jnp.where(flag_ref[2] == 0, s, (s % SIDE) * SIDE + s // SIDE)


def project_half_kernel(t_now, flag_ref, x_ref, own_ref, peer_ref, q_ref, kv_ref, wm_ref, wr_ref, nm_ref, nr_ref, sems):
    def copies(w_ref):
        found = []
        for t in range(3):
            lanes = pl.ds(t * HEAD_DIM, HEAD_DIM)
            found.append(pltpu.make_async_copy(w_ref.at[t, :, :LANES, :], wm_ref.at[:, :, lanes], sems.at[2 * t]))
            found.append(pltpu.make_async_copy(w_ref.at[t, :, LANES:, :], wr_ref.at[:, :, lanes], sems.at[2 * t + 1]))
        return found

    @pl.when(flag_ref[t_now] == 1)
    def _():
        for copy in copies(own_ref):
            copy.start()

    @pl.when(flag_ref[t_now] == 0)
    def _():
        for copy in copies(peer_ref):
            copy.start()

    low = low_lanes(ROWS)
    at = [place(flag_ref, s) for s in range(SEQ)]

    def line(s, k):
        pair = x_ref[at[s], PACK:, :].astype(F32)
        return pair[2 * k : 2 * k + 1] + pair[2 * k + 1 : 2 * k + 2]

    scale_first = [line(s, 0) for s in range(SEQ)]
    shift_first = [line(s, 2) for s in range(SEQ)]
    scale_last = [jnp.where(low[:1], line(2 * p, 1), line(2 * p + 1, 1)) for p in range(SEQ // 2)]
    shift_last = [jnp.where(low[:1], line(2 * p, 3), line(2 * p + 1, 3)) for p in range(SEQ // 2)]
    for j in range(SIDE):
        mine = pl.ds(j * ROWS, ROWS)
        rest = pl.ds(HALF + (j % 2) * ROWS, ROWS)
        total = jnp.zeros((ROWS, LANES), F32)
        square = jnp.zeros((ROWS, LANES), F32)
        total_rest = jnp.zeros((ROWS, LANES), F32)
        square_rest = jnp.zeros((ROWS, LANES), F32)
        for s in range(SEQ):
            x = x_ref[at[s], mine, :].astype(F32)
            total = total + x
            square = square + x * x
            x = x_ref[at[s], rest, :].astype(F32)
            total_rest = total_rest + x
            square_rest = square_rest + x * x
        in_half = low if j < 2 else jnp.logical_not(low)
        total = total + jnp.where(in_half, total_rest, 0.0)
        square = square + jnp.where(in_half, square_rest, 0.0)
        mean = jnp.sum(total, axis=1, keepdims=True) / WIDTH
        var = jnp.sum(square, axis=1, keepdims=True) / WIDTH - mean * mean
        rstd = lax.rsqrt(var + EPSILON)
        for s in range(SEQ):
            x = x_ref[at[s], mine, :].astype(F32)
            normed = (x - mean) * rstd * scale_first[s] + shift_first[s]
            nm_ref[mine, tile(s)] = normed.astype(BF16)
        for p in range(SEQ // 2):
            even = x_ref[at[2 * p], rest, :].astype(F32)
            odd = x_ref[at[2 * p + 1], rest, :].astype(F32)
            if j < 2:
                x = pair_lanes(low, even, odd)
            else:
                x = jnp.where(low, pltpu.roll(even, REST, 1), odd)
            normed = (x - mean) * rstd * scale_last[p] + shift_last[p]
            nr_ref[mine, tile(p)] = normed.astype(BF16)

    for copy in copies(own_ref):
        copy.wait()
    w_first = wm_ref[...].reshape(SEQ * LANES, 3 * HEAD_DIM)
    w_last = wr_ref[...].reshape(SEQ * REST, 3 * HEAD_DIM)
    qkv = jnp.dot(nm_ref[...], w_first, preferred_element_type=F32)
    qkv = qkv + jnp.dot(nr_ref[...], w_last, preferred_element_type=F32)
    qkv = qkv.astype(BF16)
    q_ref[...] = qkv[:, :HEAD_DIM]
    kv_ref[0] = qkv[:, HEAD_DIM : 2 * HEAD_DIM]
    kv_ref[1] = qkv[:, 2 * HEAD_DIM :]


def attend_half_kernel(t, flag_ref, order_ref, q_ref, kv_ref, other_ref, own_ref, got_ref, *refs):
    o_own_ref, o_peer_ref, out_ref, w_ref, cache_ref, sem, sems = refs
    leaving = []
    for whose, new_ref in enumerate((kv_ref, other_ref)):
        first = (flag_ref[2] if whose == 0 else 1 - flag_ref[2]) * SIDE
        for part in range(2):
            for n in range(SIDE):
                here = cache_ref.at[part, patch_at(order_ref, first + n), :]
                new = new_ref.at[part, n * ROWS : (n + 1) * ROWS, :]
                leaving.append(pltpu.make_async_copy(new, here, sems.at[len(leaving)]))

    @pl.when(flag_ref[t] == 1)
    def _():
        pltpu.make_async_copy(o_own_ref, w_ref, sem).start()

    @pl.when(flag_ref[t] == 0)
    def _():
        pltpu.make_async_copy(o_peer_ref, w_ref, sem).start()

    for copy in leaving:
        copy.start()

    mine = flag_ref[t] == 1
    core = flag_ref[2]

    def stale(part, j):
        peer = got_ref[patch_at(order_ref, j, CACHE + part * ALL), :]
        return jnp.where(mine, own_ref[part, patch_at(order_ref, j), :], peer)

    old, other = [], []
    for part in range(2):
        old.append([stale(part, core * SIDE + j) for j in range(SIDE)])
        kept = jnp.concatenate([stale(part, (1 - core) * SIDE + j) for j in range(SIDE)], axis=0)
        other.append(jnp.where(core == 1, other_ref[part], kept))
    queries, keys, values = [], [], []
    for j in range(SIDE):
        queries.append(q_ref[j * ROWS : (j + 1) * ROWS, :])
        for part, found in ((0, keys), (1, values)):
            parts = [kv_ref[part, : (j + 1) * ROWS, :]] + old[part][j + 1 :] + [other[part]]
            found.append(jnp.concatenate(parts, axis=0))
    for j, mixed in enumerate(softmax_mix(queries, keys, values)):
        for s in range(SIDE):
            out_ref[s, j * ROWS : (j + 1) * ROWS, :] = mixed
    pltpu.make_async_copy(o_own_ref, w_ref, sem).wait()
    for copy in leaving:
        copy.wait()


def update_half_kernel(t, flag_ref, mixed_ref, w_ref, x_ref, send_ref, got_ref, rows_out_ref, *refs):
    last = t == 1
    if last:
        hand_out_ref, held_ref, rows_ref, hand_ref, sems = refs
    else:
        new_ref, spread_ref, held_ref, rows_ref, _, sems = refs

    mixed = jnp.concatenate([mixed_ref[place(flag_ref, h)] for h in range(SEQ)], axis=1)
    held_ref[:, :SHARD] = lax.dot_general(mixed, w_ref[...], TRANSPOSED, preferred_element_type=F32)
    mods = mods_of(flag_ref, t, send_ref, got_ref).astype(F32)
    gate_first = mods[8:9] + mods[9:10]
    gate_last = mods[10:11] + mods[11:12]
    first = (x_ref[:HALF, :].astype(F32) + gate_first * held_ref[:, :LANES]).astype(BF16)
    made = pair_lanes(low_lanes(QUARTER), held_ref[:QUARTER, LANES:], held_ref[QUARTER:, LANES:])
    rest = x_ref[HALF:, :].astype(F32) + gate_last * made
    other = pltpu.roll(rest, REST, 1)
    if last:
        for n in range(SIDE):
            lines = (rest if n < 2 else other)[(n % 2) * ROWS : (n % 2 + 1) * ROWS]
            hand_ref[n, :ROWS, :] = first[n * ROWS : (n + 1) * ROWS]
            both = pair_lanes(low_lanes(ROWS // 2), lines[: ROWS // 2], lines[ROWS // 2 :])
            hand_ref[n, ROWS:, :] = both.astype(BF16)
        out = [pltpu.make_async_copy(hand_ref, hand_out_ref, sems.at[1])]
        out[0].start()
    else:
        out = []
    other = other.astype(BF16)
    rest = rest.astype(BF16)
    for n in range(SIDE):
        at = slice((n % 2) * ROWS, (n % 2 + 1) * ROWS)
        rows_ref[n, :, :LANES] = first[n * ROWS : (n + 1) * ROWS]
        rows_ref[n, :, LANES:] = rest[at] if n < 2 else other[at]
    out.append(pltpu.make_async_copy(rows_ref, rows_out_ref, sems.at[0]))
    out[-1].start()
    if not last:
        mods = mods_of(flag_ref, 1, send_ref, got_ref)
        new_ref[:HALF, :] = first
        new_ref[HALF:, :] = rest
        for s in range(SIDE):
            spread_ref[s, :HALF, :] = first
            spread_ref[s, HALF:PACK, :] = rest
            spread_ref[s, PACK:, :] = mods
    for copy in out:
        copy.wait()


def mods_kernel(gathered_ref, out_ref):
    low = low_lanes(1)
    rows = [gathered_ref[i, :MODS, :].astype(F32) for i in range(SIDE)]
    lines = []
    for k in range(3):
        for h in range(2):
            first, last = 4 * k + h, 4 * k + 2 + h
            parts = [rows[i][first : first + 1] for i in range(SIDE)]
            for m in range(SIDE // 2):
                even, odd = (rows[2 * m + e][last : last + 1] for e in range(2))
                parts.append(jnp.where(low, even, odd))
            lines.append(jnp.concatenate(parts, axis=1))
    lines.append(jnp.zeros((MODS - len(lines), WIDE), F32))
    out_ref[...] = jnp.concatenate(lines, axis=0).astype(BF16)


def spread_kernel(low_ref, high_ref, out_ref):
    for s in range(SEQ):
        out_ref[s, :PIECE, :] = low_ref[s // SIDE]
        out_ref[s, PIECE:, :] = high_ref[s // SIDE]


def unpack(even, odd):
    low = low_lanes(ROWS // 2)
    return jnp.concatenate([pair_lanes(low, even, odd), jnp.where(low, pltpu.roll(even, REST, 1), odd)], axis=0)


def project_kernel(packed, row_ref, x_ref, mods_in_ref, w_ref, below_ref, above_ref, *refs):
    across_low_ref, across_high_ref, q_ref, kv_ref, *refs = refs
    if packed:
        keep_out_ref, *refs = refs
    wm_ref, wr_ref, nm_ref, nr_ref, keep_ref, mods_ref, sems = refs
    mods_copy = pltpu.make_async_copy(mods_in_ref, mods_ref, sems.at[76])
    mods_copy.start()
    i = row_ref[0]
    half = SIDE // 2
    sources = (
        (w_ref, 0, SIDE, i),
        (below_ref, 0, SIDE, lax.rem(i + 3, SIDE)),
        (above_ref, 0, SIDE, lax.rem(i + 1, SIDE)),
        (across_low_ref, 0, half, lax.rem(i + 2, SIDE)),
        (across_high_ref, half, SIDE, lax.rem(i + 2, SIDE)),
    )
    copies = []
    for t in range(3):
        for source, first, last, h in sources:
            lanes = pl.ds(pl.multiple_of((t * SIDE + h) * HEAD_DIM, HEAD_DIM), HEAD_DIM)
            pairs = [(source.at[t, :, :, :LANES, :], wm_ref.at[first:last, :, :, lanes])]
            pairs += [(source.at[t, :, j, LANES:, :], wr_ref.at[j, first:last, :, lanes]) for j in range(SIDE)]
            copies += [pltpu.make_async_copy(a, b, sems.at[len(copies) + n]) for n, (a, b) in enumerate(pairs)]
    for copy in copies:
        copy.start()
    mods_copy.wait()
    mods = [mods_ref[j].astype(F32) for j in range(SIDE)]
    scale = [m[0:1] + m[1:2] for m in mods]
    shift = [m[2:3] + m[3:4] for m in mods]
    tiles = WIDE // LANES

    def features(g, j, k):
        if not packed:
            return x_ref[j, g * ROWS : (g + 1) * ROWS, tile(k)].astype(F32)
        if k < SIDE:
            return x_ref[k * SIDE + j, g * PIECE : g * PIECE + ROWS, :].astype(F32)
        pair = (2 * (k - SIDE) * SIDE + j, (2 * (k - SIDE) + 1) * SIDE + j)
        return unpack(*(x_ref[s, g * PIECE + ROWS : (g + 1) * PIECE, :].astype(F32) for s in pair))

    for g in range(GROUP):
        mine = pl.ds(g * ROWS, ROWS)
        total, square = (jnp.zeros((ROWS, LANES), F32) for _ in range(2))
        for j in range(SIDE):
            for k in range(tiles):
                x = features(g, j, k)
                total = total + x
                square = square + x * x
        mean = jnp.sum(total, axis=1, keepdims=True) / WIDTH
        var = jnp.sum(square, axis=1, keepdims=True) / WIDTH - mean * mean
        rstd = lax.rsqrt(var + EPSILON)
        for j in range(SIDE):
            for k in range(tiles):
                x = features(g, j, k)
                normed = ((x - mean) * rstd * scale[j][:, tile(k)] + shift[j][:, tile(k)]).astype(BF16)
                if k < SIDE:
                    nm_ref[mine, tile(k * SIDE + j)] = normed
                else:
                    nr_ref[mine, tile(j * (SIDE // 2) + k - SIDE)] = normed
        if packed:
            for k in range(tiles):
                keep_ref[mine, tile(k)] = features(g, row_ref[1], k).astype(BF16)
    kept = [pltpu.make_async_copy(keep_ref, keep_out_ref, sems.at[len(copies)])] if packed else []
    for copy in kept:
        copy.start()
    each = len(copies) // 3
    for t in range(3):
        for copy in copies[t * each : (t + 1) * each]:
            copy.wait()
        lanes = slice(t * HEADS, (t + 1) * HEADS)
        part = jnp.dot(nm_ref[...], wm_ref[:, :, :, lanes].reshape(SEQ * LANES, HEADS), preferred_element_type=F32)
        part = part + jnp.dot(nr_ref[...], wr_ref[:, :, :, lanes].reshape(SEQ * REST, HEADS), preferred_element_type=F32)
        part = part.astype(BF16)
        if t == 0:
            q_ref[...] = part
        else:
            for s in range(SIDE):
                kv_ref[s, :, (t - 1) * HEADS : t * HEADS] = part
    for copy in kept:
        copy.wait()


def load_out(i, w_ref, below_ref, above_ref, across_low_ref, across_high_ref, held_ref, sems):
    width = SEQ * HEAD_DIM
    sources = (
        (w_ref, 0, width, i),
        (below_ref, 0, width, lax.rem(i + 3, SIDE)),
        (above_ref, 0, width, lax.rem(i + 1, SIDE)),
        (across_low_ref, 0, width // 2, lax.rem(i + 2, SIDE)),
        (across_high_ref, width // 2, width, lax.rem(i + 2, SIDE)),
    )
    copies = []
    for source, begin, end, h in sources:
        first = pl.ds(pl.multiple_of(h * LANES, LANES), LANES)
        last = pl.ds(pl.multiple_of(SIDE * LANES + h * REST, REST), REST)
        for taken, rows in ((slice(0, LANES), first), (slice(LANES, SHARD), last)):
            held = held_ref.at[rows, begin:end]
            copies.append(pltpu.make_async_copy(source.at[taken, :], held, sems.at[len(copies)]))
    return copies


def attend_kernel(row_ref, order_ref, q_ref, kv_ref, stale_ref, *refs):
    *w_refs, out_ref, held_ref, cache_ref, sems = refs
    i = row_ref[0]
    copies = load_out(i, *w_refs, held_ref, sems)
    for part in range(2):
        lanes = pl.ds(pl.multiple_of(part * HEADS + i * HEAD_DIM, HEAD_DIM), HEAD_DIM)
        for n in range(SIDE):
            for half in range(GROUP):
                new = kv_ref.at[n, half * ROWS : (half + 1) * ROWS, lanes]
                own = cache_ref.at[part, patch_at(order_ref, half * SIDE + n), :]
                copies.append(pltpu.make_async_copy(new, own, sems.at[len(copies)]))
    for copy in copies:
        copy.start()
    for pair in range(SIDE // 2):
        where, queries, keys, values = [], [], [], []
        for h in (2 * pair, 2 * pair + 1):
            new, old = [], []
            for part in range(2):
                lanes = tile(part * SIDE + h)
                halves = [slice(g * ROWS, (g + 1) * ROWS) for g in range(GROUP)]
                new.append([kv_ref[n % SIDE, halves[n // SIDE], lanes] for n in range(PATCHES)])
                old.append([stale_ref[h, patch_at(order_ref, n, MODS + part * ALL), :] for n in range(PATCHES)])
            for g in range(GROUP):
                where.append((halves[g], tile(h)))
                queries.append(q_ref[halves[g], tile(h)])
                for part, found in ((0, keys), (1, values)):
                    rows = [jnp.where(n <= i + SIDE * g, new[part][n], old[part][n]) for n in range(PATCHES)]
                    found.append(jnp.concatenate(rows, axis=0))
        for (rows, lanes), mixed in zip(where, softmax_mix(queries, keys, values), strict=True):
            for s in range(SIDE):
                out_ref[s, rows, lanes] = mixed
    for copy in copies:
        copy.wait()


def update_kernel(last, mixed_ref, held_ref, x_in_ref, mods_in_ref, *refs):
    if not last:
        out_ref, *refs = refs
    part_ref, x_ref, mods_ref, made_ref, cut_ref, sems = refs
    copies = []
    copies.append(pltpu.make_async_copy(x_in_ref, x_ref, sems.at[len(copies)]))
    copies.append(pltpu.make_async_copy(mods_in_ref, mods_ref, sems.at[len(copies)]))
    for copy in copies:
        copy.start()
    mixed = jnp.concatenate([mixed_ref[h % SIDE, :, tile(h // SIDE)] for h in range(SEQ)], axis=1)
    for copy in copies:
        copy.wait()
    made = lax.dot_general(mixed, held_ref[...], TRANSPOSED, preferred_element_type=F32)
    mods = mods_ref[...].astype(F32)
    new = x_ref[...].astype(F32) + (mods[4:5] + mods[5:6]) * made
    out = []
    if not last:
        made_ref[...] = new.astype(BF16)
        out.append(pltpu.make_async_copy(made_ref, out_ref, sems.at[0]))
        out[0].start()
    for n in range(SIDE):
        rest = new[:, tile(SIDE + n // 2)]
        cut_ref[n, :, :LANES] = new[:, tile(n)].astype(BF16)
        cut_ref[n, :, LANES:] = (rest if n % 2 == 0 else pltpu.roll(rest, REST, 1)).astype(BF16)
    out.append(pltpu.make_async_copy(cut_ref, part_ref, sems.at[1]))
    out[-1].start()
    for copy in out:
        copy.wait()


def finish_kernel(order_ref, low_ref, high_ref, out_ref, rows_ref):
    for half, x_ref in enumerate((low_ref, high_ref)):
        for n in range(SIDE):
            rows_ref[patch_at(order_ref, half * SIDE + n), :] = x_ref[n].astype(F32)
    out_ref[...] = rows_ref[...].T[:SHARD, :].astype(BF16)


def blank(*shapes):
    return pl.pallas_call(lambda *refs: None, out_shape=shapes, out_specs=(ANY,) * len(shapes), name="blank")()


def body(latents, patch_order, timestep, mod_table, w_qkv, w_out, kv_cache):
    sections = lax.axis_size("section")
    section = lax.axis_index("section")
    position = section % CHAIN
    core = (section % 2).astype(jnp.int32)
    seq = lax.axis_index("seq").astype(jnp.int32)
    row = jnp.stack([seq // SIDE, seq % SIDE])
    w_own = jnp.transpose(w_qkv[0], (1, 0, 2))
    o_own = jnp.transpose(w_out[0], (1, 0))
    cache_own = kv_cache[0]
    mod_now = lax.dynamic_index_in_dim(mod_table, timestep[0], 0, keepdims=False)[0]

    def swap(value):
        return lax.ppermute(value, "section", [(s, s ^ 1) for s in range(sections) if s % CHAIN < 2])

    def exchange(value, groups):
        return lax.all_to_all(value, "seq", 0, 0, axis_index_groups=groups)

    def shift(value, by):
        pairs = [(s, (s + SIDE * by) % SEQ) for s in range(SEQ)]
        return lax.ppermute(value, "seq", pairs)

    def by_core(value, even, odd):
        groups = [[s * SEQ + d for d in g] for s in range(sections) for g in (odd if s % 2 else even)]
        return lax.all_to_all(value, ("section", "seq"), 0, 0, axis_index_groups=groups)

    def gather_mixed(spread):
        near = by_core(spread, ALONG_Z, ALONG_X)
        far = by_core(jnp.broadcast_to(near[None], (SIDE,) + near.shape), ALONG_X, ALONG_Z)
        return far.reshape((SEQ,) + near.shape[1:])

    def gather(value, groups):
        return exchange(jnp.broadcast_to(value[None], (SIDE,) + value.shape), groups)

    cache_shape = shaped(2, ALL, HEAD_DIM)
    rows_shape, kv_shape = shaped(SIDE, ROWS, 2 * LANES), shaped(2, HALF, HEAD_DIM)
    hand_shape, x_shape, parts_shape = shaped(SIDE, PIECE, LANES), shaped(PART, WIDE), shaped(SIDE, PART, 2 * LANES)

    flags = jnp.stack([core == 0, core == 1, core]).astype(jnp.int32)
    flags, mod_now = lax.optimization_barrier((flags, mod_now))
    own, send = call(
        pack_kernel,
        "pack",
        (shaped(PACK, LANES), shaped(CACHE + 2 * ALL, LANES)),
        [SMEM, VMEM, VMEM, VMEM],
        patch_order,
        jnp.transpose(latents[0], (1, 0)),
        mod_now,
        cache_own,
        scratch=[pltpu.VMEM((ALL, 2 * LANES), F32)],
    )
    own, send, w_own, o_own = lax.optimization_barrier((own, send, w_own, o_own))
    got, w_peer, o_peer = swap(send), swap(w_own), swap(o_own)
    got, w_peer, o_peer = lax.optimization_barrier((got, w_peer, o_peer))

    spread_shape = shaped(SIDE, PACK + MODS, LANES)

    def first_blocks(own, send, got, w_peer, o_peer):
        shapes = shaped(PACK, LANES), spread_shape
        x, spread = call(start_kernel, "start", shapes, [SMEM, VMEM, VMEM, VMEM], flags, own, send, got)
        gathered = gather_mixed(spread)
        kept = []
        for t in range(2):
            q, kv = call(
                functools.partial(project_half_kernel, t),
                "project_half",
                (shaped(HALF, HEAD_DIM), kv_shape),
                [SMEM, VMEM, ANY, ANY],
                flags,
                gathered,
                w_own.reshape(3, SEQ, SHARD, HEAD_DIM),
                w_peer.reshape(3, SEQ, SHARD, HEAD_DIM),
                scratch=[
                    pltpu.VMEM((SEQ, LANES, 3 * HEAD_DIM), BF16),
                    pltpu.VMEM((SEQ, REST, 3 * HEAD_DIM), BF16),
                    pltpu.VMEM((HALF, SEQ * LANES), BF16),
                    pltpu.VMEM((HALF, SEQ * REST), BF16),
                    pltpu.SemaphoreType.DMA((6,)),
                ],
            )
            kv_other = swap(kv)
            mixed, w_now, cache = call(
                functools.partial(attend_half_kernel, t),
                "attend_half",
                (shaped(SIDE, HALF, HEAD_DIM), shaped(*o_own.shape), cache_shape),
                [SMEM, SMEM, VMEM, VMEM, VMEM, VMEM, VMEM, ANY, ANY],
                flags,
                patch_order,
                q,
                kv,
                kv_other,
                cache_own,
                got,
                o_own,
                o_peer,
                scratch=[pltpu.SemaphoreType.DMA, pltpu.SemaphoreType.DMA((4 * SIDE,))],
                outside=(2,),
            )
            heads = gather_mixed(mixed)
            last = t == 1
            results = call(
                functools.partial(update_half_kernel, t),
                "update_half",
                (rows_shape,) + ((hand_shape,) if last else (shaped(PACK, LANES), spread_shape)),
                [SMEM, VMEM, VMEM, VMEM, VMEM, VMEM],
                flags,
                heads,
                w_now,
                x,
                send,
                got,
                scratch=[
                    pltpu.VMEM((HALF, 2 * LANES), F32),
                    pltpu.VMEM(rows_shape.shape, BF16),
                    pltpu.VMEM(hand_shape.shape, BF16),
                    pltpu.SemaphoreType.DMA((2,)),
                ],
                outside=(0, 1) if last else (0,),
            )
            if not last:
                x, gathered = results[1], gather_mixed(results[2])
            kept.append((results[0], cache))
        return results[1], kept

    half_width = SEQ * HEAD_DIM // 2

    def prepare(small):
        w = w_own.reshape(3, SIDE, SIDE, SHARD, HEAD_DIM)
        w_near, o, small = lax.optimization_barrier(((shift(w, 1), shift(w, -1)), o_own, small))
        w_far = shift(w_near[0][:, : SIDE // 2], 1), shift(w_near[1][:, SIDE // 2 :], -1)
        o_near = shift(o, 1), shift(o, -1)
        small = gather(small, ALONG_X)
        mods = call(mods_kernel, "mods", shaped(MODS, WIDE), [VMEM], small, mib=4)
        others = gather(mods, ALONG_Z), small, mods
        w_far, o_near, others = lax.optimization_barrier((w_far, o_near, others))
        o_far = shift(o_near[0][:, :half_width], 1), shift(o_near[1][:, half_width:], -1)
        mods_all, small, mods = others
        return w_near + w_far, o_near + o_far, small, mods, mods_all

    def no_weights(small):
        side, half = (shaped(3, n, SIDE, SHARD, HEAD_DIM) for n in (SIDE, SIDE // 2))
        whole, part = (shaped(SHARD, n) for n in (2 * half_width, half_width))
        shapes = (side, side, half, half, whole, whole, part, part)
        shapes += (shaped(SIDE, *small.shape), shaped(MODS, WIDE), shaped(SIDE, MODS, WIDE))
        made = blank(*shapes)
        return tuple(made[:4]), tuple(made[4:8]), *made[8:]

    def later_block(x, gathered, w_others, o_others, small, mods, mods_all):
        packed = x is None
        q, kv, *keep = call(
            functools.partial(project_kernel, packed),
            "project",
            (shaped(PART, HEADS), shaped(SIDE, PART, 2 * HEADS)) + (x_shape,) * packed,
            [SMEM, VMEM] + [ANY] * 6,
            row,
            gathered,
            mods_all,
            w_own.reshape(3, SIDE, SIDE, SHARD, HEAD_DIM),
            *w_others,
            scratch=[
                pltpu.VMEM((SIDE, SIDE, LANES, 3 * HEADS), BF16),
                pltpu.VMEM((SIDE, SIDE, REST, 3 * HEADS), BF16),
                pltpu.VMEM((PART, SEQ * LANES), BF16),
                pltpu.VMEM((PART, SEQ * REST), BF16),
                pltpu.VMEM(x_shape.shape, BF16),
                pltpu.VMEM((SIDE, MODS, WIDE), BF16),
                pltpu.SemaphoreType.DMA((77,)),
            ],
            outside=(2,),
            mib=20,
        )
        x = keep[0] if packed else x
        mixed, held, cache = call(
            attend_kernel,
            "attend",
            (shaped(SIDE, PART, HEADS), shaped(WIDE, SEQ * HEAD_DIM), cache_shape),
            [SMEM, SMEM, VMEM, VMEM, VMEM] + [ANY] * 5,
            row,
            patch_order,
            q,
            exchange(kv, ALONG_X),
            small,
            o_own,
            *o_others,
            scratch=[pltpu.SemaphoreType.DMA((26,))],
            outside=(2,),
        )
        made = call(
            functools.partial(update_kernel, not packed),
            "update",
            (x_shape,) * packed + (parts_shape,),
            [VMEM, VMEM, ANY, ANY],
            exchange(mixed, ALONG_Z),
            held,
            x,
            mods,
            scratch=[
                pltpu.VMEM(x_shape.shape, BF16),
                pltpu.VMEM((MODS, WIDE), BF16),
                pltpu.VMEM(x_shape.shape, BF16),
                pltpu.VMEM(parts_shape.shape, BF16),
                pltpu.SemaphoreType.DMA((2,)),
            ],
            outside=(0, 1),
        )
        return *made, cache

    def second_block(low, high, weights):
        spread = call(spread_kernel, "spread", shaped(SEQ, 2 * PIECE, LANES), [VMEM, VMEM], low, high)
        return later_block(None, lax.all_to_all(spread, "seq", 0, 0), *weights)

    def third_block(x, weights):
        return later_block(x, gather(x, ALONG_Z), *weights)

    early = position < 2
    def not_here(*_):
        hand, *both = blank(hand_shape, rows_shape, cache_shape, rows_shape, cache_shape)
        return hand, [tuple(both[:2]), tuple(both[2:])]

    hand, kept = lax.cond(early, first_blocks, not_here, own, send, got, w_peer, o_peer)
    weights = lax.cond(early, no_weights, prepare, send[PACK:])
    hand, weights = lax.optimization_barrier((hand, weights))
    low = lax.ppermute(hand, "section", [(s, s + 2) for s in range(sections) if s % CHAIN == 0])
    high = lax.ppermute(hand, "section", [(s, s + 1) for s in range(sections) if s % CHAIN == 1])
    state = blank(x_shape, parts_shape, cache_shape)
    state = lax.cond(
        position == 2,
        lambda low, high, state, weights: second_block(low, high, weights),
        lambda low, high, state, weights: tuple(state),
        low,
        high,
        tuple(state),
        weights,
    )
    arrived = lax.ppermute(state[0], "section", [(s, s + 1) for s in range(sections) if s % CHAIN == 2])
    state = lax.cond(
        position == 3,
        lambda x, state, weights: third_block(x, weights),
        lambda x, state, weights: tuple(state),
        arrived,
        tuple(state[1:]),
        weights,
    )

    def finish_early(state, kept):
        (rows0, cache0), (rows1, cache1) = kept
        first = core == 0
        mine, theirs = jnp.where(first, rows0, rows1), jnp.where(first, rows1, rows0)
        other = swap(theirs)
        return jnp.where(first, mine, other), jnp.where(first, other, mine), jnp.where(first, cache0, cache1)

    def finish_late(state, kept):
        parts, cache = state
        rows = exchange(parts, ALONG_X)
        return rows[:, :ROWS], rows[:, ROWS:], cache

    rows_low, rows_high, cache = lax.cond(early, finish_early, finish_late, state, kept)
    out_t = call(
        finish_kernel,
        "finish",
        shaped(SHARD, ALL),
        [SMEM, VMEM, VMEM],
        patch_order,
        rows_low,
        rows_high,
        scratch=[pltpu.VMEM((ALL, 2 * LANES), F32)],
    )
    return jnp.transpose(out_t, (1, 0))[None], cache[None]


def solution(mesh):
    return jax.shard_map(
        body,
        mesh=mesh,
        in_specs=(
            P("section", None, "seq"),
            P(),
            P(),
            P(None, "section", None, "seq"),
            P("section", None, None, "seq"),
            P("section", None, "seq"),
            P("section", None, None, "seq"),
        ),
        out_specs=(P("section", None, "seq"), P("section", None, None, "seq")),
        check_vma=False,
    )
```
